128 devices in a mesh: dp: 32 (over z, y_hi, x), tensor: 4 (over y_lo, core).
Axes of the slice: x: 4, y: 4 (y_hi: 2, y_lo: 2; y = y_hi * 2 + y_lo), z: 4, core: 2. Of those that a mesh axis runs over, the one named last changes fastest.
Arguments:
- tokens: bfloat16 [16384, 1024], P(('dp', 'tensor')), may hold values from -6 to 6
- cotangent: bfloat16 [16384, 1024], P(('dp', 'tensor')), may hold values from -6 to 6
- lengths: int32 [32, 4], P('dp'), may hold values from 1 to 509, as said below
- small: float32 [5, 1024], P(None, ('dp', 'tensor')), may hold values from -1.5 to 1.5
- mix_in: float32 [3, 1024, 1024], P(None, 'dp', 'tensor'), may hold values from -0.1875 to 0.1875
- mix_out: float32 [1024, 1024], P('dp', 'tensor'), may hold values from -0.1875 to 0.1875
- ffn_gate_up: float32 [2, 1024, 4608], P(None, 'dp', 'tensor'), may hold values from -0.1875 to 0.1875
- ffn_down: float32 [1024, 4608], P('dp', 'tensor'), may hold values from -0.09375 to 0.09375
- small_first: float32 [5, 1024], P(None, ('dp', 'tensor'))
- small_second: float32 [5, 1024], P(None, ('dp', 'tensor'))
- in_first: float32 [3, 1024, 1024], P(None, 'dp', 'tensor')
- in_second: float32 [3, 1024, 1024], P(None, 'dp', 'tensor')
- out_first: float32 [1024, 1024], P('dp', 'tensor')
- out_second: float32 [1024, 1024], P('dp', 'tensor')
- gate_up_first: float32 [2, 1024, 4608], P(None, 'dp', 'tensor')
- gate_up_second: float32 [2, 1024, 4608], P(None, 'dp', 'tensor')
- down_first: float32 [1024, 4608], P('dp', 'tensor')
- down_second: float32 [1024, 4608], P('dp', 'tensor')
Outputs:
- block_out: bfloat16 [16384, 1024], P(('dp', 'tensor'))
- tokens_grad: float32 [16384, 1024], P(('dp', 'tensor'))
- small_moment: float32 [5, 1024], P(None, ('dp', 'tensor'))
- small_square: float32 [5, 1024], P(None, ('dp', 'tensor'))
- small_new: float32 [5, 1024], P(None, ('dp', 'tensor'))
- in_moment: float32 [3, 1024, 1024], P(None, 'dp', 'tensor')
- in_square: float32 [3, 1024, 1024], P(None, 'dp', 'tensor')
- in_new: float32 [3, 1024, 1024], P(None, 'dp', 'tensor')
- out_moment: float32 [1024, 1024], P('dp', 'tensor')
- out_square: float32 [1024, 1024], P('dp', 'tensor')
- out_new: float32 [1024, 1024], P('dp', 'tensor')
- gate_up_moment: float32 [2, 1024, 4608], P(None, 'dp', 'tensor')
- gate_up_square: float32 [2, 1024, 4608], P(None, 'dp', 'tensor')
- gate_up_new: float32 [2, 1024, 4608], P(None, 'dp', 'tensor')
- down_moment: float32 [1024, 4608], P('dp', 'tensor')
- down_square: float32 [1024, 4608], P('dp', 'tensor')
- down_new: float32 [1024, 4608], P('dp', 'tensor')
The draws below stay inside these ranges and needn't reach their ends.
Inputs may be any that keep to these rules, and one draw needn't show every extreme that they name: The lengths of a group sum to at most 512; in every group one sequence covers rows from the first quarter to the last quarter of the group.
All inputs are finite; a program needn't handle non-finite values.
Results may differ from the reference program's by a relative error of at most 0.04.
Values may be sent and summed in bfloat16 or wider, within the bound.
A program may use at most 128 MiB of HBM per device.

```python
import math
import jax
import jax.numpy as jnp
from jax import lax

D = 1024
FF = 4608
TOK_DEV = 128
SEQS = 4
STEP = 10
TOKENS = 16384
N_DP = 32
N_TENSOR = 4


def moment_first(key, shape, scale):
    return scale * 0.111 * jnp.clip(jax.random.normal(key, shape, jnp.float32), -4.0, 4.0)


def moment_second(key, shape, scale):
    return scale * scale * 0.0526 * jnp.exp(jax.random.uniform(key, shape, jnp.float32, 0.0, math.log(4.0)))


def small_scale():
    return jnp.array([1.7, 0.84, 1.2, 1.2, 1.2], jnp.float32)[:, None] * math.sqrt(TOKENS)


def draw_lengths(key, part):
    key = jax.random.fold_in(key, 11)
    rows = TOK_DEV * N_TENSOR
    key_pad, key_short, key_full, key_slot = jax.random.split(key, 4)
    pads = jax.random.randint(key_pad, (N_DP,), 0, rows // 16 + 1)
    shorts = jax.random.randint(key_short, (N_DP, SEQS - 1), 1, rows // 64 + 1)
    full_group = jax.random.randint(key_full, (), 0, N_DP)
    is_full = jnp.arange(N_DP) == full_group
    pads = jnp.where(is_full, 0, pads)
    shorts = jnp.where(is_full[:, None], 1, shorts)
    longest = rows - pads - jnp.sum(shorts, axis=1)
    slot = jax.random.randint(key_slot, (N_DP,), 0, SEQS)
    index = jnp.arange(SEQS)
    rank = index[None, :] - (index[None, :] > slot[:, None]).astype(jnp.int32)
    picked = jnp.take_along_axis(shorts, jnp.clip(rank, 0, SEQS - 2), axis=1)
    return jnp.where(index[None, :] == slot[:, None], longest[:, None], picked).astype(jnp.int32)


def draw_small(key, part):
    key = jax.random.fold_in(key, 12)
    key_gain, key_tap = jax.random.split(key)
    gains = 1.0 + 0.15 * jnp.clip(jax.random.normal(key_gain, (2, D), jnp.float32), -3.0, 3.0)
    taps = 0.5 * jnp.clip(jax.random.normal(key_tap, (3, D), jnp.float32), -3.0, 3.0)
    return jnp.concatenate([gains, taps], axis=0)


def draw_small_first(key, part):
    key = jax.random.fold_in(key, 13)
    return moment_first(key, (5, D), small_scale())


def draw_small_second(key, part):
    key = jax.random.fold_in(key, 14)
    return moment_second(key, (5, D), small_scale())


def draw_in_first(key, part):
    key = jax.random.fold_in(key, 15)
    return moment_first(key, (3, D, D), math.sqrt(TOKENS))


def draw_in_second(key, part):
    key = jax.random.fold_in(key, 16)
    return moment_second(key, (3, D, D), math.sqrt(TOKENS))


def draw_out_first(key, part):
    key = jax.random.fold_in(key, 17)
    return moment_first(key, (D, D), math.sqrt(TOKENS))


def draw_out_second(key, part):
    key = jax.random.fold_in(key, 18)
    return moment_second(key, (D, D), math.sqrt(TOKENS))


def draw_gate_up_first(key, part):
    key = jax.random.fold_in(key, 19)
    return moment_first(key, (2, D, FF), 0.3 * math.sqrt(TOKENS))


def draw_gate_up_second(key, part):
    key = jax.random.fold_in(key, 20)
    return moment_second(key, (2, D, FF), 0.3 * math.sqrt(TOKENS))


def draw_down_first(key, part):
    key = jax.random.fold_in(key, 21)
    return moment_first(key, (D, FF), 0.6 * math.sqrt(TOKENS))


def draw_down_second(key, part):
    key = jax.random.fold_in(key, 22)
    return moment_second(key, (D, FF), 0.6 * math.sqrt(TOKENS))


def level_of(own_key, dims, pieces, smallest, top_value):
    loudness, own = 1.0, jax.random.fold_in(own_key, 6)
    for axis_at, shards_of in pieces:
        steps = jnp.exp(jax.random.uniform(jax.random.fold_in(own, axis_at), (shards_of,), jnp.float32, smallest / len(pieces), top_value / len(pieces)))
        loudness = loudness * jnp.repeat(steps, dims[axis_at] // shards_of).reshape([-1 if axis == axis_at else 1 for axis in range(len(dims))])
    return loudness


def normal_values(stream_key, shape, width, limit, cuts=(), kind=jnp.bfloat16):
    values = width * jax.random.normal(stream_key, shape, jnp.float32)
    if cuts:
        values = values * level_of(stream_key, shape, cuts, -0.22, 0.18)
    return jnp.clip(values, -limit, limit).astype(kind)


def setup_inputs(seed: int = 0) -> dict:
    key_of = jax.random.split(jax.random.key(seed), 19)
    tokens = normal_values(key_of[0], (TOKENS, D), 1.0, 6.0, ((0, 128),))
    cotangent = normal_values(key_of[1], (TOKENS, D), 1.0, 6.0, ((0, 128),))
    lengths = draw_lengths(jax.random.fold_in(key_of[18], 71), 0)
    small = draw_small(jax.random.fold_in(key_of[18], 71), 0)
    mix_in = normal_values(key_of[4], (3, D, D), D ** -0.5, 0.1875, ((1, 32), (2, 4)), jnp.float32)
    mix_out = normal_values(key_of[5], (D, D), D ** -0.5, 0.1875, ((0, 32), (1, 4)), jnp.float32)
    ffn_gate_up = normal_values(key_of[6], (2, D, FF), D ** -0.5, 0.1875, ((1, 32), (2, 4)), jnp.float32)
    ffn_down = normal_values(key_of[7], (D, FF), FF ** -0.5, 0.09375, ((0, 32), (1, 4)), jnp.float32)
    small_first = draw_small_first(jax.random.fold_in(key_of[18], 71), 0)
    small_second = draw_small_second(jax.random.fold_in(key_of[18], 71), 0)
    in_first = draw_in_first(jax.random.fold_in(key_of[18], 71), 0)
    in_second = draw_in_second(jax.random.fold_in(key_of[18], 71), 0)
    out_first = draw_out_first(jax.random.fold_in(key_of[18], 71), 0)
    out_second = draw_out_second(jax.random.fold_in(key_of[18], 71), 0)
    gate_up_first = draw_gate_up_first(jax.random.fold_in(key_of[18], 71), 0)
    gate_up_second = draw_gate_up_second(jax.random.fold_in(key_of[18], 71), 0)
    down_first = draw_down_first(jax.random.fold_in(key_of[18], 71), 0)
    down_second = draw_down_second(jax.random.fold_in(key_of[18], 71), 0)
    return dict(tokens=tokens, cotangent=cotangent, lengths=lengths, small=small, mix_in=mix_in, mix_out=mix_out, ffn_gate_up=ffn_gate_up, ffn_down=ffn_down, small_first=small_first, small_second=small_second, in_first=in_first, in_second=in_second, out_first=out_first, out_second=out_second, gate_up_first=gate_up_first, gate_up_second=gate_up_second, down_first=down_first, down_second=down_second)


NORM_EPSILON = 1e-05
BETA_FIRST = 0.9
BETA_SECOND = 0.95
ADAM_EPSILON = 1e-08
DECAY_RATE = 0.1
RATE_PROJ = 0.1
RATE_DOWN = 0.045
RATE_SMALL = 0.6
HIGHEST = lax.Precision.HIGHEST

@jax.custom_vjp
def low(v):
    return lax.optimization_barrier(v.astype(jnp.bfloat16)).astype(jnp.float32)

@jax.custom_vjp
def low_back(v):
    return v

def low_keep(v):
    return (low(v), None)

def low_pass(kept, grad):
    return (grad,)

def back_keep(v):
    return (v, None)

def back_low(kept, grad):
    return (low(grad),)
low.defvjp(low_keep, low_pass)
low_back.defvjp(back_keep, back_low)

def seq_layout(lens, rows):
    lens = lens.astype(jnp.int32)
    offsets = jnp.cumsum(lens) - lens
    total = jnp.sum(lens)
    starts = jnp.concatenate([offsets, total[None]]).astype(jnp.int32)
    places = jnp.arange(rows, dtype=jnp.int32)
    before = starts[None, :] <= places[:, None]
    seg_start = lax.optimization_barrier(jnp.max(jnp.where(before, starts[None, :], 0), axis=1)).astype(jnp.int32)
    return (places - seg_start, places < total)

def shift_down(values, steps):
    return jnp.pad(values[:-steps], ((steps, 0), (0, 0)))

def block_forward(params, rows_in, one_tap, two_tap):
    small, mix_in, mix_out, ffn_gate_up, ffn_down = params
    inv_one = lax.rsqrt(lax.optimization_barrier(jnp.mean(rows_in * rows_in, axis=1, keepdims=True)) + NORM_EPSILON)
    normed_one = low(rows_in * inv_one * small[0])
    proj = low_back(jnp.einsum('rd,jdc->jrc', normed_one, low(mix_in), precision=HIGHEST))
    mixed = proj[0] * proj[2]
    conv_out = small[2] * mixed + small[3] * shift_down(mixed, 1) * one_tap + small[4] * shift_down(mixed, 2) * two_tap
    gated = low(proj[1] * conv_out)
    mix_sum = low_back(jnp.einsum('rc,dc->rd', gated, low(mix_out), precision=HIGHEST))
    mid = rows_in + mix_sum
    inv_two = lax.rsqrt(lax.optimization_barrier(jnp.mean(mid * mid, axis=1, keepdims=True)) + NORM_EPSILON)
    normed_two = low(mid * inv_two * small[1])
    gate_up = low_back(jnp.einsum('rd,jdf->jrf', normed_two, low(ffn_gate_up), precision=HIGHEST))
    hidden = low(jax.nn.silu(gate_up[0]) * gate_up[1])
    ffn_sum = jnp.einsum('rf,df->rd', hidden, low(ffn_down), precision=HIGHEST)
    return mid + ffn_sum

def adam_step(weight, grad, first, second, rate):
    first_new = BETA_FIRST * first + (1.0 - BETA_FIRST) * grad
    second_new = BETA_SECOND * second + (1.0 - BETA_SECOND) * grad * grad
    first_hat = first_new / (1.0 - BETA_FIRST ** STEP)
    second_hat = second_new / (1.0 - BETA_SECOND ** STEP)
    weight_new = weight - rate * (first_hat / (jnp.sqrt(second_hat) + ADAM_EPSILON) + DECAY_RATE * weight)
    return (first_new, second_new, weight_new)

def reference(tokens, cotangent, lengths, small, mix_in, mix_out, ffn_gate_up, ffn_down, small_first, small_second, in_first, in_second, out_first, out_second, gate_up_first, gate_up_second, down_first, down_second):
    group_rows = TOK_DEV * N_TENSOR
    params = (small, mix_in, mix_out, ffn_gate_up, ffn_down)
    token_groups = tokens.astype(jnp.float32).reshape(N_DP, group_rows, D)
    cot_groups = cotangent.astype(jnp.float32).reshape(N_DP, group_rows, D)

    def per_group(totals, inputs):
        rows_in, cot_rows, lens = inputs
        distance, live = seq_layout(lens, group_rows)
        one_tap = (distance >= 1)[:, None].astype(jnp.float32)
        two_tap = (distance >= 2)[:, None].astype(jnp.float32)
        result, pullback = jax.vjp(lambda pars, rows: block_forward(pars, rows, one_tap, two_tap), params, rows_in)
        par_grads, row_grads = pullback(cot_rows * live[:, None].astype(jnp.float32))
        totals = jax.tree.map(lambda left, right: left + right, totals, par_grads)
        return (totals, (result.astype(jnp.bfloat16), row_grads))
    zeros = jax.tree.map(jnp.zeros_like, params)
    totals, (outputs, row_grads) = lax.scan(per_group, zeros, (token_groups, cot_groups, lengths))
    small_grad, in_grad, out_grad, gate_up_grad, down_grad = totals
    small_moment, small_square, small_new = adam_step(small, small_grad, small_first, small_second, RATE_SMALL)
    in_moment, in_square, in_new = adam_step(mix_in, in_grad, in_first, in_second, RATE_PROJ)
    out_moment, out_square, out_new = adam_step(mix_out, out_grad, out_first, out_second, RATE_PROJ)
    gate_up_moment, gate_up_square, gate_up_new = adam_step(ffn_gate_up, gate_up_grad, gate_up_first, gate_up_second, RATE_PROJ)
    down_moment, down_square, down_new = adam_step(ffn_down, down_grad, down_first, down_second, RATE_DOWN)
    return (outputs.reshape(TOKENS, D), row_grads.reshape(TOKENS, D), small_moment, small_square, small_new, in_moment, in_square, in_new, out_moment, out_square, out_new, gate_up_moment, gate_up_square, gate_up_new, down_moment, down_square, down_new)
```

```python
import functools

import jax
import jax.numpy as jnp
from jax import lax
from jax.experimental import pallas as pl
from jax.experimental.pallas import tpu as pltpu
from jax.sharding import PartitionSpec as P

STEP = 10
NORM_EPSILON = 1e-05
BETA_FIRST = 0.9
BETA_SECOND = 0.95
ADAM_EPSILON = 1e-08
DECAY_RATE = 0.1
RATE_PROJ = 0.1
RATE_DOWN = 0.045
RATE_SMALL = 0.6

MESH = pl.DeviceIdType.MESH
F32 = jnp.float32
BF16 = jnp.bfloat16

D = 1024
ROWS = 512
BLOCK = 128
CH = 256
HID = 1152
TILE = 128
TILES = HID // TILE
OUT_AT = 3 * CH
GU_AT = 4 * CH
DOWN_AT = GU_AT + 2 * HID
WIDE = DOWN_AT + HID
PARTS = ((0, GU_AT), (GU_AT, 2 * HID), (DOWN_AT, HID))
NZ, NY, NX, SHARD = 4, 2, 4, 32
HALF = SHARD // 2


def mm(a, b):
    return lax.dot_general(a, b, (((1,), (0,)), ((), ())), preferred_element_type=F32)


def mm_nt(a, b):
    return lax.dot_general(a, b, (((1,), (1,)), ((), ())), preferred_element_type=F32)


def loop(n, body):
    lax.fori_loop(0, n, lambda i, carry: (body(i), carry)[1], 0)


def at_lane(i, width):
    return pl.ds(pl.multiple_of(i * width, width), width)


class Links:
    def __init__(self, send, recv):
        self.send, self.recv, self.used, self.open = send, recv, 0, []

    def take(self, n=1):
        first = self.used
        self.used += n
        return first

    def copy(self, src, dst, to, slot):
        return pltpu.make_async_remote_copy(
            src_ref=src,
            dst_ref=dst,
            send_sem=self.send.at[slot],
            recv_sem=self.recv.at[slot],
            device_id=to,
            device_id_type=MESH,
        )

    def push(self, src, dst, to):
        c = self.copy(src, dst, to, self.take())
        c.start()
        self.open.append(c)
        return c


def arrived(copies):
    for c in copies:
        c.wait_recv()


def train_kernel(
    lens,
    tok_in,
    cot_in,
    small_in,
    win,
    wout,
    wgu,
    wdn,
    bo_out,
    tg_out,
    gs_out,
    sg_out,
    w,
    g,
    tok,
    cot,
    one,
    two,
    rmid,
    masks,
    pj,
    conv,
    gated,
    gp,
    gu,
    hid,
    gg,
    mid,
    gmid,
    sml,
    st,
    sr,
    sm,
    sgr,
    gr,
    gc,
    gacc,
    ps,
    pr,
    po,
    qs,
    qr,
    r2s1,
    r2s2z,
    r2s2x,
    r1s1,
    r1s2,
    ry,
    send_sem,
    recv_sem,
):
    dp = lax.axis_index("dp")
    t = lax.axis_index("tensor")
    z, yh, x = dp // 8, (dp // 4) % 2, dp % 4
    ty, tc = t // 2, t % 2
    zp, zm, zo = (z + 1) % 4, (z + 3) % 4, (z + 2) % 4
    xp, xm, xo = (x + 1) % 4, (x + 3) % 4, (x + 2) % 4

    def at(zz, yy, xx):
        return (zz * 8 + yy * 4 + xx, t)

    to_y = at(z, 1 - yh, x)
    to_xp, to_xm = at(z, yh, xp), at(z, yh, xm)
    to_zp, to_zm = at(zp, yh, x), at(zm, yh, x)
    x1 = x + 1 - 2 * (x % 2)
    z1 = z + 1 - 2 * (z % 2)
    to_x1, to_x3 = at(z, yh, x1), at(z, yh, 3 - x)
    to_z1, to_z3 = at(z1, yh, x), at(3 - z, yh, x)
    to_core = (dp, ty * 2 + 1 - tc)
    to_far = (dp, (1 - ty) * 2 + tc)
    links = Links(send_sem, recv_sem)

    for j in range(3):
        w[z, yh, x, :, j * CH : (j + 1) * CH] = win[j].astype(BF16)
    w[z, yh, x, :, OUT_AT : OUT_AT + CH] = wout[...].astype(BF16)
    for i in range(TILES):
        for j in range(2):
            lo = GU_AT + (2 * i + j) * TILE
            w[z, yh, x, :, lo : lo + TILE] = wgu[j, :, i * TILE : (i + 1) * TILE].astype(BF16)
    w[z, yh, x, :, DOWN_AT:WIDE] = wdn[...].astype(BF16)
    tok[ty, tc] = tok_in[...]
    st[0] = small_in[...]

    row = lax.broadcasted_iota(jnp.int32, (ROWS, TILE), 0)
    start = jnp.zeros((ROWS, TILE), jnp.int32)
    run = jnp.int32(0)
    for k in range(lens.shape[1]):
        run = run + lens[0, k]
        start = jnp.where(row >= run, run, start)
    dist = row - start
    masks[0] = jnp.where(dist >= 1, 1.0, 0.0)
    masks[1] = jnp.where(dist >= 2, 1.0, 0.0)
    my_row = lax.broadcasted_iota(jnp.int32, (BLOCK, D), 0) + t * BLOCK
    cot[ty, tc] = jnp.where(my_row < run, cot_in[...].astype(F32), 0.0).astype(BF16)

    barrier = pltpu.get_barrier_semaphore()
    peers = (to_y, to_xp, to_xm, to_zp, to_zm, to_core, to_far)
    for to in peers:
        pl.semaphore_signal(barrier, inc=1, device_id=to, device_id_type=MESH)
    pl.semaphore_wait(barrier, len(peers))

    lo_half, hi_half = pl.ds(0, HALF), pl.ds(HALF, HALF)

    def cols(part):
        return pl.ds(PARTS[part][0], PARTS[part][1])

    def same(ref, to):
        return links.push(ref, ref, to)

    def wy(p):
        return same(w.at[z, yh, x, :, cols(p)], to_y)

    def w1a(p):
        a, b = w.at[z, :, x, lo_half, cols(p)], w.at[z, :, x, hi_half, cols(p)]
        return [same(a, to_xp), same(a, to_xm), same(b, to_zp), same(b, to_zm)]

    def w1b(p):
        return [
            same(w.at[z, 0, xm, lo_half, cols(p)], to_xp),
            same(w.at[z, 1, xp, lo_half, cols(p)], to_xm),
            same(w.at[zm, 0, x, hi_half, cols(p)], to_zp),
            same(w.at[zp, 1, x, hi_half, cols(p)], to_zm),
        ]

    def w2a(p):
        a, b = w.at[z, :, :, lo_half, cols(p)], w.at[:, :, x, hi_half, cols(p)]
        return [same(a, to_zp), same(a, to_zm), same(b, to_xp), same(b, to_xm)]

    def w2b(p):
        return [
            same(w.at[zm, 0, :, lo_half, cols(p)], to_zp),
            same(w.at[zp, 1, :, lo_half, cols(p)], to_zm),
            same(w.at[:, 0, xm, hi_half, cols(p)], to_xp),
            same(w.at[:, 1, xp, hi_half, cols(p)], to_xm),
        ]

    def rows_start(ref):
        mine = ref.at[ty, tc]
        return [same(mine, to_far), same(mine, to_core)]

    def rows_relay(ref, copies):
        copies[0].wait_recv()
        copies.append(same(ref.at[1 - ty, tc], to_core))

    def rows_wait(copies):
        arrived(copies[1:])

    def sum_start(u, lhs, lo, k):
        first = links.take(NZ)

        def step(i):
            wt = w[i, :, :, :, lo : lo + k].reshape(D // NZ, k)
            a = lhs[:, 1 - tc].reshape(2 * BLOCK, k)
            ps[u, i] = mm_nt(a, wt).astype(BF16).reshape(2, BLOCK, CH)
            links.copy(ps.at[u, i], pr.at[u, i], to_core, first + i).start()
            b = lhs[:, tc].reshape(2 * BLOCK, k)
            po[u, i] = mm_nt(b, wt).reshape(2, BLOCK, CH)

        loop(NZ, step)
        links.open += [links.copy(ps.at[u, i], pr.at[u, i], to_core, first + i) for i in range(NZ)]
        return first

    def sum_cross(u, first):
        second = links.take(NZ)

        def step(i):
            links.copy(ps.at[u, i], pr.at[u, i], to_core, first + i).wait_recv()
            other = po[u, i, 1 - ty] + pr[u, i, 1 - ty].astype(F32)
            qs[u, i] = other.astype(BF16)
            links.copy(qs.at[u, i], qr.at[u, i], to_far, second + i).start()
            po[u, i, ty] = po[u, i, ty] + pr[u, i, ty].astype(F32)

        loop(NZ, step)
        links.open += [links.copy(qs.at[u, i], qr.at[u, i], to_far, second + i) for i in range(NZ)]
        return second

    def sum_wait(u, second):
        for i in range(NZ):
            links.copy(qs.at[u, i], qr.at[u, i], to_far, second + i).wait_recv()

    def sum_rows(u, lo, n):
        return jnp.concatenate(
            [po[u, i, ty, pl.ds(lo, n), :] + qr[u, i, pl.ds(lo, n), :].astype(F32) for i in range(NZ)],
            axis=1,
        )

    def add_to(dst, src):
        dst[...] = (dst[...].astype(F32) + src[...].astype(F32)).astype(BF16)

    def g2a(p):
        c = cols(p)
        return [
            links.push(g.at[zo, 0, :, lo_half, c], r2s1.at[0, 0, :, :, c], to_zm),
            links.push(g.at[zo, 1, :, lo_half, c], r2s1.at[0, 1, :, :, c], to_zp),
            links.push(g.at[:, 0, xo, hi_half, c], r2s1.at[1, 0, :, :, c], to_xm),
            links.push(g.at[:, 1, xo, hi_half, c], r2s1.at[1, 1, :, :, c], to_xp),
        ]

    def g2b(p, copies):
        c = cols(p)
        out = []
        for k, (y, zz, to) in enumerate(((0, zm, to_zm), (1, zp, to_zp))):
            copies[k].wait_recv()
            loop(4, lambda i: add_to(g.at[zz, y, i, lo_half, c], r2s1.at[0, y, i, :, c]))
            out.append(links.push(g.at[zz, :, :, lo_half, c], r2s2z.at[y, :, :, :, c], to))
        for k, (y, xx, to) in enumerate(((0, xm, to_xm), (1, xp, to_xp))):
            copies[2 + k].wait_recv()
            loop(4, lambda i: add_to(g.at[i, y, xx, hi_half, c], r2s1.at[1, y, i, :, c]))
            out.append(links.push(g.at[:, :, xx, hi_half, c], r2s2x.at[y, :, :, :, c], to))
        return out

    def add_two(dst, a, b):
        total = dst[...].astype(F32) + a[...].astype(F32) + b[...].astype(F32)
        dst[...] = total.astype(BF16)

    def g1a(p, copies):
        c = cols(p)
        arrived(copies[:2])
        loop(
            8,
            lambda i: add_two(
                g.at[z, i // 4, i % 4, lo_half, c],
                r2s2z.at[0, i // 4, i % 4, :, c],
                r2s2z.at[1, i // 4, i % 4, :, c],
            ),
        )
        out = [
            links.push(g.at[z, 0, xo, lo_half, c], r1s1.at[0, 0, :, c], to_xm),
            links.push(g.at[z, 1, xo, lo_half, c], r1s1.at[0, 1, :, c], to_xp),
        ]
        arrived(copies[2:])
        loop(
            8,
            lambda i: add_two(
                g.at[i // 2, i % 2, x, hi_half, c],
                r2s2x.at[0, i // 2, i % 2, :, c],
                r2s2x.at[1, i // 2, i % 2, :, c],
            ),
        )
        return out + [
            links.push(g.at[zo, 0, x, hi_half, c], r1s1.at[1, 0, :, c], to_zm),
            links.push(g.at[zo, 1, x, hi_half, c], r1s1.at[1, 1, :, c], to_zp),
        ]

    def g1b(p, copies):
        c = cols(p)
        out = []
        for k, (y, xx, to) in enumerate(((0, xm, to_xm), (1, xp, to_xp))):
            copies[k].wait_recv()
            add_to(g.at[z, y, xx, lo_half, c], r1s1.at[0, y, :, c])
            out.append(links.push(g.at[z, :, xx, lo_half, c], r1s2.at[0, y, :, :, c], to))
        for k, (y, zz, to) in enumerate(((0, zm, to_zm), (1, zp, to_zp))):
            copies[2 + k].wait_recv()
            add_to(g.at[zz, y, x, hi_half, c], r1s1.at[1, y, :, c])
            out.append(links.push(g.at[zz, :, x, hi_half, c], r1s2.at[1, y, :, :, c], to))
        return out

    def gy(p, copies):
        c = cols(p)
        arrived(copies)
        for h, rows in enumerate((lo_half, hi_half)):
            loop(
                2,
                lambda y: add_two(
                    g.at[z, y, x, rows, c], r1s2.at[h, 0, y, :, c], r1s2.at[h, 1, y, :, c]
                ),
            )
        return links.push(g.at[z, 1 - yh, x, :, c], ry.at[:, c], to_y)

    def gend(p, copy):
        c = cols(p)
        copy.wait_recv()
        gs_out[:, c] = g[z, yh, x, :, c].astype(F32) + ry[:, c].astype(F32)

    s_far = links.push(st.at[0], sr.at[0], to_far)
    y0 = wy(0)
    tok_c = rows_start(tok)
    y1 = wy(1)
    y2 = wy(2)
    s_far.wait_recv()
    st[1] = st[0] + sr[0]
    s_core = links.push(st.at[1], sr.at[1], to_core)
    y0.wait_recv()
    a1a = w1a(0)
    s_core.wait_recv()
    st[2] = st[1] + sr[1]
    s_x1 = links.push(st.at[2], sr.at[2], to_x1)
    rows_relay(tok, tok_c)
    arrived(a1a)
    a1b = w1b(0)
    s_x1.wait_recv()
    st[3] = st[2] + sr[2]
    s_x3 = links.push(st.at[3], sr.at[3], to_x3)
    y1.wait_recv()
    b1a = w1a(1)
    s_x3.wait_recv()
    sm[z, yh] = st[3] + sr[3]
    s_y = same(sm.at[z, yh], to_y)
    arrived(a1b)
    a2a = w2a(0)
    y2.wait_recv()
    c1a = w1a(2)
    s_y.wait_recv()
    s_z1 = same(sm.at[z], to_z1)
    cot_c = rows_start(cot)
    s_z1.wait_recv()
    s_z3 = same(sm.at[pl.ds((z // 2) * 2, 2)], to_z3)
    arrived(b1a)
    b1b = w1b(1)
    s_z3.wait_recv()
    for k in range(8):
        sml[:, k * TILE : (k + 1) * TILE] = sm[k // 2, k % 2]
    rows_wait(tok_c)

    def norm_in(i):
        a, b, r = i // 8, (i // 4) % 2, (i % 4) * 32
        v = tok[a, b, pl.ds(r, 32), :].astype(F32)
        inv = lax.rsqrt(jnp.mean(v * v, axis=1, keepdims=True) + NORM_EPSILON)
        one[a, b, pl.ds(r, 32), :] = (v * inv * sml[0:1, :]).astype(BF16)

    loop(16, norm_in)
    arrived(a2a)
    a2b = w2b(0)
    arrived(b1b)
    b2a = w2a(1)
    arrived(c1a)
    c1b = w1b(2)
    rows_relay(cot, cot_c)
    arrived(a2b)

    def proj(j):
        pj[j] = mm(one[...].reshape(ROWS, D), w[:, :, :, :, at_lane(j, CH)].reshape(D, CH))

    loop(3, proj)
    arrived(c1b)
    c2a = w2a(2)

    def taps(k, lanes):
        return sml[2 + k : 3 + k, lanes]

    for q in range(2):
        lanes = slice(q * TILE, (q + 1) * TILE)
        own = at_lane(t * 2 + q, TILE)
        mixed = pj[0, :, lanes] * pj[2, :, lanes]
        before_one = pltpu.roll(mixed, 1, 0) * masks[0]
        before_two = pltpu.roll(mixed, 2, 0) * masks[1]
        v = taps(0, own) * mixed + taps(1, own) * before_one + taps(2, own) * before_two
        conv[:, lanes] = v
        gated[:, :, :, lanes] = (pj[1, :, lanes] * v).astype(BF16).reshape(2, 2, BLOCK, TILE)

    m_first = sum_start(0, gated, OUT_AT, CH)
    m_second = sum_cross(0, m_first)
    sum_wait(0, m_second)

    def norm_mid(i):
        r = i * 32
        v = tok[ty, tc, pl.ds(r, 32), :].astype(F32) + sum_rows(0, r, 32)
        mid[pl.ds(r, 32), :] = v
        inv = lax.rsqrt(jnp.mean(v * v, axis=1, keepdims=True) + NORM_EPSILON)
        two[ty, tc, pl.ds(r, 32), :] = (v * inv * sml[1:2, :]).astype(BF16)

    loop(4, norm_mid)
    two_c = rows_start(two)
    arrived(b2a)
    b2b = w2b(1)
    rows_relay(two, two_c)
    rows_wait(two_c)
    rows_wait(cot_c)
    arrived(b2b)

    def gate_up(i):
        lanes = pl.ds(pl.multiple_of(GU_AT + i * CH, CH), CH)
        v = mm(two[...].reshape(ROWS, D), w[:, :, :, :, lanes].reshape(D, CH))
        gate, up = v[:, :TILE], v[:, TILE:]
        s = jax.nn.sigmoid(gate)
        act = gate * s
        hid[:, :, :, at_lane(i, TILE)] = (act * up).astype(BF16).reshape(2, 2, BLOCK, TILE)
        gu[i, :, :TILE] = up * s * (1.0 + gate * (1.0 - s))
        gu[i, :, TILE:] = act

    loop(TILES, gate_up)
    arrived(c2a)
    c2b = w2b(2)

    def wide(v):
        return v.reshape(NY, NX, SHARD, v.shape[1])

    def down_grad(i):
        a = cot[:, :, :, at_lane(i, CH)].reshape(ROWS, CH).T
        g[i, :, :, :, DOWN_AT:WIDE] = wide(mm(a, hid[...].reshape(ROWS, HID)).astype(BF16))

    loop(NZ, down_grad)
    gc2a = g2a(2)
    arrived(c2b)

    def back_tile(k, gh):
        v = gu[k]
        gg[:, :, :, at_lane(2 * k, TILE)] = (gh * v[:, :TILE]).astype(BF16).reshape(2, 2, BLOCK, TILE)
        gg[:, :, :, at_lane(2 * k + 1, TILE)] = (
            (gh * v[:, TILE:]).astype(BF16).reshape(2, 2, BLOCK, TILE)
        )

    def grad_hidden(i):
        lanes = pl.ds(pl.multiple_of(DOWN_AT + i * CH, TILE), CH)
        v = mm(cot[...].reshape(ROWS, D), w[:, :, :, :, lanes].reshape(D, CH))
        back_tile(2 * i, v[:, :TILE])
        back_tile(2 * i + 1, v[:, TILE:])

    loop(TILES // 2, grad_hidden)
    back_tile(
        TILES - 1,
        mm(cot[...].reshape(ROWS, D), w[:, :, :, :, WIDE - TILE : WIDE].reshape(D, TILE)),
    )
    n_first = sum_start(1, gg, GU_AT, 2 * HID)
    n_second = sum_cross(1, n_first)

    def gate_up_grad(i):
        a = two[:, :, :, at_lane(i, CH)].reshape(ROWS, CH).T
        for q in range(3):
            lo = q * 3 * CH
            b = gg[:, :, :, lo : lo + 3 * CH].reshape(ROWS, 3 * CH)
            g[i, :, :, :, GU_AT + lo : GU_AT + lo + 3 * CH] = wide(mm(a, b).astype(BF16))

    loop(NZ, gate_up_grad)
    gb2a = g2a(1)
    sum_wait(1, n_second)
    gacc[...] = jnp.zeros_like(gacc)

    def norm_two_back(i):
        r = i * 32
        gn = sum_rows(1, r, 32)
        v = mid[pl.ds(r, 32), :]
        inv = lax.rsqrt(jnp.mean(v * v, axis=1, keepdims=True) + NORM_EPSILON)
        unit = v * inv
        gacc[1:2, :] += jnp.sum(gn * unit, axis=0, keepdims=True)
        scaled = gn * sml[1:2, :]
        inner = jnp.mean(scaled * unit, axis=1, keepdims=True)
        out = cot[ty, tc, pl.ds(r, 32), :].astype(F32) + inv * (scaled - unit * inner)
        gmid[pl.ds(r, 32), :] = out
        rmid[ty, tc, pl.ds(r, 32), :] = out.astype(BF16)

    loop(4, norm_two_back)
    mid_c = rows_start(rmid)
    gc2b = g2b(2, gc2a)
    rows_relay(rmid, mid_c)
    o_first = sum_start(2, hid, DOWN_AT, HID)
    rows_wait(mid_c)
    gc1a = g1a(2, gc2b)
    gb2b = g2b(1, gb2a)

    pj_c = mm(rmid[...].reshape(ROWS, D), w[:, :, :, :, OUT_AT : OUT_AT + CH].reshape(D, CH))
    pg = pj_c
    for q in range(2):
        lanes = slice(q * TILE, (q + 1) * TILE)
        own = at_lane(t * 2 + q, TILE)
        gate_b, gate_c, values = pj[0, :, lanes], pj[1, :, lanes], pj[2, :, lanes]
        mixed = gate_b * values
        gv = pg[:, lanes]
        grad_c = gv * conv[:, lanes]
        grad_conv = gv * gate_c
        one_grad, two_grad = grad_conv * masks[0], grad_conv * masks[1]
        gacc[2:3, own] = jnp.sum(grad_conv * mixed, axis=0, keepdims=True)
        gacc[3:4, own] = jnp.sum(one_grad * pltpu.roll(mixed, 1, 0), axis=0, keepdims=True)
        gacc[4:5, own] = jnp.sum(two_grad * pltpu.roll(mixed, 2, 0), axis=0, keepdims=True)
        grad_mixed = (
            taps(0, own) * grad_conv
            + taps(1, own) * pltpu.roll(one_grad, ROWS - 1, 0)
            + taps(2, own) * pltpu.roll(two_grad, ROWS - 2, 0)
        )
        for j, v in enumerate((grad_mixed * values, grad_c, grad_mixed * gate_b)):
            lo = j * CH + q * TILE
            gp[:, :, :, lo : lo + TILE] = v.astype(BF16).reshape(2, 2, BLOCK, TILE)

    i_first = sum_start(3, gp, 0, 3 * CH)

    def mix_grad(i):
        a = one[:, :, :, at_lane(i, CH)].reshape(ROWS, CH).T
        g[i, :, :, :, :OUT_AT] = wide(mm(a, gp[...].reshape(ROWS, 3 * CH)).astype(BF16))
        b = rmid[:, :, :, at_lane(i, CH)].reshape(ROWS, CH).T
        g[i, :, :, :, OUT_AT:GU_AT] = wide(mm(b, gated[...].reshape(ROWS, CH)).astype(BF16))

    loop(NZ, mix_grad)
    ga2a = g2a(0)
    i_second = sum_cross(3, i_first)
    gc1b = g1b(2, gc1a)
    o_second = sum_cross(2, o_first)
    sum_wait(3, i_second)

    def norm_one_back(i):
        r = i * 32
        gn = sum_rows(3, r, 32)
        v = tok[ty, tc, pl.ds(r, 32), :].astype(F32)
        inv = lax.rsqrt(jnp.mean(v * v, axis=1, keepdims=True) + NORM_EPSILON)
        unit = v * inv
        gacc[0:1, :] += jnp.sum(gn * unit, axis=0, keepdims=True)
        scaled = gn * sml[0:1, :]
        inner = jnp.mean(scaled * unit, axis=1, keepdims=True)
        tg_out[pl.ds(r, 32), :] = gmid[pl.ds(r, 32), :] + inv * (scaled - unit * inner)

    loop(4, norm_one_back)
    for k in range(8):
        sgr[k // 2, k % 2] = gacc[:, k * TILE : (k + 1) * TILE]
    pair = (z // 2) * 2
    u_z3 = links.push(sgr.at[pl.ds(2 - pair, 2)], gr.at[pl.ds(0, 2)], to_z3)
    ga2b = g2b(0, ga2a)
    u_z3.wait_recv()
    sgr[pl.ds(pair, 2)] = sgr[pl.ds(pair, 2)] + gr[0:2]
    u_z1 = links.push(sgr.at[z1], gr.at[2], to_z1)
    gb1a = g1a(1, gb2b)
    u_z1.wait_recv()
    sgr[z] = sgr[z] + gr[2]
    u_y = links.push(sgr.at[z, 1 - yh], gc.at[0], to_y)
    gcy = gy(2, gc1b)
    gb1b = g1b(1, gb1a)
    u_y.wait_recv()
    gc[1] = sgr[z, yh] + gc[0]
    u_x1 = links.push(gc.at[1], gc.at[2], to_x1)
    ga1a = g1a(0, ga2b)
    u_x1.wait_recv()
    gc[3] = gc[1] + gc[2]
    u_x3 = links.push(gc.at[3], gc.at[4], to_x3)
    ga1b = g1b(0, ga1a)
    gby = gy(1, gb1b)
    u_x3.wait_recv()
    gc[5] = gc[3] + gc[4]
    u_far = links.push(gc.at[5], gc.at[6], to_far)
    sum_wait(2, o_second)

    def out_rows(i):
        r = i * 32
        bo_out[pl.ds(r, 32), :] = (mid[pl.ds(r, 32), :] + sum_rows(2, r, 32)).astype(BF16)

    loop(4, out_rows)
    u_far.wait_recv()
    gc[7] = gc[5] + gc[6]
    u_core = links.push(gc.at[7], gc.at[8], to_core)
    gay = gy(0, ga1b)
    gend(2, gcy)
    gend(1, gby)
    u_core.wait_recv()
    sg_out[...] = gc[7] + gc[8]
    gend(0, gay)
    for c in links.open:
        c.wait_send()


N_COPIES = 176


def train_call(lengths, tokens, cotangent, small_tile, mix_in, mix_out, gate_up, down):
    vmem = pl.BlockSpec(memory_space=pltpu.VMEM)
    rows = (2, 2, BLOCK)
    return pl.pallas_call(
        train_kernel,
        out_shape=(
            jax.ShapeDtypeStruct((BLOCK, D), BF16),
            jax.ShapeDtypeStruct((BLOCK, D), F32),
            jax.ShapeDtypeStruct((SHARD, WIDE), F32),
            jax.ShapeDtypeStruct((8, TILE), F32),
        ),
        in_specs=[pl.BlockSpec(memory_space=pltpu.SMEM)] + [vmem] * 7,
        out_specs=[vmem] * 4,
        scratch_shapes=[
            pltpu.VMEM((NZ, NY, NX, SHARD, WIDE), BF16),
            pltpu.VMEM((NZ, NY, NX, SHARD, WIDE), BF16),
            pltpu.VMEM(rows + (D,), BF16),
            pltpu.VMEM(rows + (D,), BF16),
            pltpu.VMEM(rows + (D,), BF16),
            pltpu.VMEM(rows + (D,), BF16),
            pltpu.VMEM(rows + (D,), BF16),
            pltpu.VMEM((2, ROWS, TILE), F32),
            pltpu.VMEM((3, ROWS, CH), F32),
            pltpu.VMEM((ROWS, CH), F32),
            pltpu.VMEM(rows + (CH,), BF16),
            pltpu.VMEM(rows + (3 * CH,), BF16),
            pltpu.VMEM((TILES, ROWS, CH), F32),
            pltpu.VMEM(rows + (HID,), BF16),
            pltpu.VMEM(rows + (2 * HID,), BF16),
            pltpu.VMEM((BLOCK, D), F32),
            pltpu.VMEM((BLOCK, D), F32),
            pltpu.VMEM((8, D), F32),
            pltpu.VMEM((4, 8, TILE), F32),
            pltpu.VMEM((4, 8, TILE), F32),
            pltpu.VMEM((NZ, NY, 8, TILE), F32),
            pltpu.VMEM((NZ, NY, 8, TILE), F32),
            pltpu.VMEM((3, NY, 8, TILE), F32),
            pltpu.VMEM((9, 8, TILE), F32),
            pltpu.VMEM((8, D), F32),
            pltpu.VMEM((4, NZ, 2, BLOCK, CH), BF16),
            pltpu.VMEM((4, NZ, 2, BLOCK, CH), BF16),
            pltpu.VMEM((4, NZ, 2, BLOCK, CH), F32),
            pltpu.VMEM((4, NZ, BLOCK, CH), BF16),
            pltpu.VMEM((4, NZ, BLOCK, CH), BF16),
            pltpu.VMEM((2, 2, 4, HALF, WIDE), BF16),
            pltpu.VMEM((2, NY, NX, HALF, WIDE), BF16),
            pltpu.VMEM((2, NZ, NY, HALF, WIDE), BF16),
            pltpu.VMEM((2, 2, HALF, WIDE), BF16),
            pltpu.VMEM((2, 2, 2, HALF, WIDE), BF16),
            pltpu.VMEM((SHARD, WIDE), BF16),
            pltpu.SemaphoreType.DMA((N_COPIES,)),
            pltpu.SemaphoreType.DMA((N_COPIES,)),
        ],
        compiler_params=pltpu.CompilerParams(
            collective_id=0, has_side_effects=True, vmem_limit_bytes=63 * 1024 * 1024
        ),
        cost_estimate=pl.CostEstimate(
            flops=6 * ROWS * D * WIDE, bytes_accessed=8 * 1024 * 1024, transcendentals=ROWS * HID
        ),
    )(lengths, tokens, cotangent, small_tile, mix_in, mix_out, gate_up, down)


def adam_step(weight, grad, first, second, rate):
    first_new = BETA_FIRST * first + (1.0 - BETA_FIRST) * grad
    second_new = BETA_SECOND * second + (1.0 - BETA_SECOND) * grad * grad
    first_hat = first_new / (1.0 - BETA_FIRST**STEP)
    second_hat = second_new / (1.0 - BETA_SECOND**STEP)
    weight_new = weight - rate * (
        first_hat / (jnp.sqrt(second_hat) + ADAM_EPSILON) + DECAY_RATE * weight
    )
    return (first_new, second_new, weight_new)


def adam_kernel(bo, tg, gs, sgrad, *refs):
    small, mix_in, mix_out, gate_up, down = refs[0:5]
    moments = refs[5:15]
    bo_new, tg_new = refs[15:17]
    outs = refs[17:]
    bo_new[...] = bo[...]
    tg_new[...] = tg[...]

    def put(k, where, grad, weight, rate):
        found = adam_step(weight[where], grad, moments[2 * k][where], moments[2 * k + 1][where], rate)
        for ref, value in zip(outs[3 * k : 3 * k + 3], found):
            ref[where] = value

    put(0, ..., sgrad[...], small, RATE_SMALL)
    for j in range(3):
        put(1, j, gs[:, j * CH : (j + 1) * CH], mix_in, RATE_PROJ)
    put(2, ..., gs[:, OUT_AT:GU_AT], mix_out, RATE_PROJ)
    for i in range(TILES):
        for j in range(2):
            lo = GU_AT + (2 * i + j) * TILE
            put(
                3,
                (j, slice(None), slice(i * TILE, (i + 1) * TILE)),
                gs[:, lo : lo + TILE],
                gate_up,
                RATE_PROJ,
            )
    put(4, ..., gs[:, DOWN_AT:WIDE], down, RATE_DOWN)


def per_device(
    tokens,
    cotangent,
    lengths,
    small,
    mix_in,
    mix_out,
    ffn_gate_up,
    ffn_down,
    small_first,
    small_second,
    in_first,
    in_second,
    out_first,
    out_second,
    gate_up_first,
    gate_up_second,
    down_first,
    down_second,
):
    place = ((lax.axis_index("dp") % 4) * 4 + lax.axis_index("tensor")) * 8
    tile = lax.dynamic_update_slice(jnp.zeros((8, TILE), F32), small, (0, place))
    bo, tg, gs, sg = train_call(
        lengths, tokens, cotangent, tile, mix_in, mix_out, ffn_gate_up, ffn_down
    )
    sgrad = lax.dynamic_slice(sg, (0, place), small.shape)
    weights = (small, mix_in, mix_out, ffn_gate_up, ffn_down)
    moments = (
        small_first,
        small_second,
        in_first,
        in_second,
        out_first,
        out_second,
        gate_up_first,
        gate_up_second,
        down_first,
        down_second,
    )
    out_shape = [jax.ShapeDtypeStruct(v.shape, v.dtype) for v in (bo, tg)]
    for v in weights:
        out_shape += [jax.ShapeDtypeStruct(v.shape, v.dtype)] * 3
    vmem = pl.BlockSpec(memory_space=pltpu.VMEM)
    return tuple(
        pl.pallas_call(
            adam_kernel,
            out_shape=out_shape,
            in_specs=[vmem] * 19,
            out_specs=[vmem] * 17,
            compiler_params=pltpu.CompilerParams(vmem_limit_bytes=32 * 1024 * 1024),
        )(bo, tg, gs, sgrad, *weights, *moments)
    )


def solution(mesh):
    rows = P(("dp", "tensor"), None)
    small = P(None, ("dp", "tensor"))
    deep = P(None, "dp", "tensor")
    flat = P("dp", "tensor")
    in_specs = (rows, rows, P("dp", None), small, deep, flat, deep, flat)
    in_specs += (small,) * 2 + (deep,) * 2 + (flat,) * 2 + (deep,) * 2 + (flat,) * 2
    out_specs = (rows, rows) + (small,) * 3 + (deep,) * 3 + (flat,) * 3 + (deep,) * 3 + (flat,) * 3
    return jax.shard_map(
        per_device, mesh=mesh, in_specs=in_specs, out_specs=out_specs, check_vma=False
    )
```

```python
import functools

import jax
import jax.numpy as jnp
from jax import lax
from jax.experimental import pallas as pl
from jax.experimental.pallas import tpu as pltpu
from jax.sharding import PartitionSpec as P

STEP = 10
NORM_EPSILON = 1e-05
BETA_FIRST = 0.9
BETA_SECOND = 0.95
ADAM_EPSILON = 1e-08
DECAY_RATE = 0.1
RATE_PROJ = 0.1
RATE_DOWN = 0.045
RATE_SMALL = 0.6

MESH = pl.DeviceIdType.MESH
F32 = jnp.float32
BF16 = jnp.bfloat16

D = 1024
ROWS = 512
BLOCK = 128
CH = 256
HID = 1152
TILE = 128
TILES = HID // TILE
OUT_AT = 3 * CH
GU_AT = 4 * CH
DOWN_AT = GU_AT + 2 * HID
WIDE = DOWN_AT + HID
FIRST = TILES // 2
GU_PARTS = ((0, FIRST), (FIRST, TILES - FIRST))
PARTS = (
    (0, GU_AT),
    (GU_AT, FIRST * CH),
    (GU_AT + FIRST * CH, (TILES - FIRST) * CH),
    (DOWN_AT, HID),
)
NZ, NY, NX, SHARD = 4, 2, 4, 32
HALF = SHARD // 2


def mm(a, b):
    return lax.dot_general(a, b, (((1,), (0,)), ((), ())), preferred_element_type=F32)


def mm_nt(a, b):
    return lax.dot_general(a, b, (((1,), (1,)), ((), ())), preferred_element_type=F32)


def loop(n, body):
    lax.fori_loop(0, n, lambda i, carry: (body(i), carry)[1], 0)


def at_lane(i, width):
    return pl.ds(pl.multiple_of(i * width, width), width)


def adam_step(weight, grad, first, second, rate):
    first_new = BETA_FIRST * first + (1.0 - BETA_FIRST) * grad
    second_new = BETA_SECOND * second + (1.0 - BETA_SECOND) * grad * grad
    first_hat = first_new / (1.0 - BETA_FIRST**STEP)
    second_hat = second_new / (1.0 - BETA_SECOND**STEP)
    weight_new = weight - rate * (
        first_hat / (jnp.sqrt(second_hat) + ADAM_EPSILON) + DECAY_RATE * weight
    )
    return (first_new, second_new, weight_new)


class Links:
    def __init__(self, send, recv):
        self.send, self.recv, self.used, self.open = send, recv, 0, []

    def take(self, n=1):
        first = self.used
        self.used += n
        return first

    def copy(self, src, dst, to, slot):
        return pltpu.make_async_remote_copy(
            src_ref=src,
            dst_ref=dst,
            send_sem=self.send.at[slot],
            recv_sem=self.recv.at[slot],
            device_id=to,
            device_id_type=MESH,
        )

    def push(self, src, dst, to):
        c = self.copy(src, dst, to, self.take())
        c.start()
        self.open.append(c)
        return c


def arrived(copies):
    for c in copies:
        c.wait_recv()


def train_kernel(*refs):
    lens, tok_in, cot_in = refs[:3]
    state_in = refs[3:18]
    bo_out, tg_out = refs[18:20]
    state_out = refs[20:35]
    train_body(lens, tok_in, cot_in, state_in, bo_out, tg_out, state_out, *refs[35:])


def train_body(
    lens,
    tok_in,
    cot_in,
    state_in,
    bo_out,
    tg_out,
    state_out,
    state_small,
    state_in_w,
    state_out_w,
    state_gu,
    state_down,
    bo,
    tg,
    local_sem,
    w,
    g,
    tok,
    cot,
    one,
    two,
    rmid,
    masks,
    pj,
    conv,
    gated,
    gp,
    gu,
    hid,
    gg,
    mid,
    gmid,
    sml,
    st,
    sr,
    sm,
    sgr,
    gr,
    gc,
    gacc,
    invs,
    ps,
    pr,
    po,
    qs,
    qr,
    r2s1,
    r2s2z,
    r2s2x,
    r1s1,
    r1s2,
    ry,
    send_sem,
    recv_sem,
):
    dp = lax.axis_index("dp")
    t = lax.axis_index("tensor")
    z, yh, x = dp // 8, (dp // 4) % 2, dp % 4
    ty, tc = t // 2, t % 2
    zp, zm, zo = (z + 1) % 4, (z + 3) % 4, (z + 2) % 4
    xp, xm, xo = (x + 1) % 4, (x + 3) % 4, (x + 2) % 4

    def at(zz, yy, xx):
        return (zz * 8 + yy * 4 + xx, t)

    to_y = at(z, 1 - yh, x)
    to_xp, to_xm = at(z, yh, xp), at(z, yh, xm)
    to_zp, to_zm = at(zp, yh, x), at(zm, yh, x)
    to_xo, to_zo = at(z, yh, xo), at(zo, yh, x)
    to_core = (dp, ty * 2 + 1 - tc)
    to_far = (dp, (1 - ty) * 2 + tc)
    to_across = (dp, (1 - ty) * 2 + 1 - tc)
    links = Links(send_sem, recv_sem)

    barrier = pltpu.get_barrier_semaphore()
    peers = (to_y, to_xp, to_xm, to_xo, to_zp, to_zm, to_zo, to_core, to_far, to_across)
    for to in peers:
        pl.semaphore_signal(barrier, inc=1, device_id=to, device_id_type=MESH)

    state = (state_small, state_in_w, state_out_w, state_gu, state_down)
    n_local = 0
    loads = {}
    for key, src, dst in (
        [((k, 0), state_in[k], state[k].at[0]) for k in range(5)]
        + [("tok", tok_in, tok.at[ty, tc]), ("cot", cot_in, cot.at[ty, tc])]
        + [((k, j), state_in[3 + 2 * k + j + 1], state[k].at[j]) for k in range(5) for j in (1, 2)]
    ):
        loads[key] = pltpu.make_async_copy(src, dst, local_sem.at[n_local])
        loads[key].start()
        n_local += 1
    stores = []

    def store(src, dst):
        c = pltpu.make_async_copy(src, dst, local_sem.at[n_local + len(stores)])
        c.start()
        stores.append(c)

    row = lax.broadcasted_iota(jnp.int32, (ROWS, TILE), 0)
    start = jnp.zeros((ROWS, TILE), jnp.int32)
    run = jnp.int32(0)
    for k in range(lens.shape[1]):
        run = run + lens[0, k]
        start = jnp.where(row >= run, run, start)
    dist = row - start
    masks[0] = jnp.where(dist >= 1, 1.0, 0.0)
    masks[1] = jnp.where(dist >= 2, 1.0, 0.0)

    place = ((dp % 4) * 4 + t) * 8
    st[0] = jnp.zeros((8, TILE), F32)
    loads[0, 0].wait()
    st[0, 0:5, 0:8] = state_small[0]
    st[0] = pltpu.roll(st[0], place, 1)
    loads[1, 0].wait()
    for j in range(3):
        w[z, yh, x, :, j * CH : (j + 1) * CH] = state_in_w[0, j].astype(BF16)
    loads[2, 0].wait()
    w[z, yh, x, :, OUT_AT : OUT_AT + CH] = state_out_w[0].astype(BF16)
    loads["tok"].wait()
    pl.semaphore_wait(barrier, len(peers))

    lo_half, hi_half = pl.ds(0, HALF), pl.ds(HALF, HALF)

    def cols(part):
        return pl.ds(PARTS[part][0], PARTS[part][1])

    def same(ref, to):
        return links.push(ref, ref, to)

    def wy(p):
        return same(w.at[z, yh, x, :, cols(p)], to_y)

    def w1a(p):
        a, b = w.at[z, :, x, lo_half, cols(p)], w.at[z, :, x, hi_half, cols(p)]
        return [same(a, to_xp), same(a, to_xm), same(b, to_zp), same(b, to_zm)]

    def w1b(p):
        return [
            same(w.at[z, 0, xm, lo_half, cols(p)], to_xp),
            same(w.at[z, 1, xp, lo_half, cols(p)], to_xm),
            same(w.at[zm, 0, x, hi_half, cols(p)], to_zp),
            same(w.at[zp, 1, x, hi_half, cols(p)], to_zm),
        ]

    def w2a(p):
        a, b = w.at[z, :, :, lo_half, cols(p)], w.at[:, :, x, hi_half, cols(p)]
        return [same(a, to_zp), same(a, to_zm), same(b, to_xp), same(b, to_xm)]

    def w2b(p):
        return [
            same(w.at[zm, 0, :, lo_half, cols(p)], to_zp),
            same(w.at[zp, 1, :, lo_half, cols(p)], to_zm),
            same(w.at[:, 0, xm, hi_half, cols(p)], to_xp),
            same(w.at[:, 1, xp, hi_half, cols(p)], to_xm),
        ]

    def rows_start(ref):
        mine = ref.at[ty, tc]
        return [same(mine, to_far), same(mine, to_core)]

    def rows_relay(ref, copies):
        copies[0].wait_recv()
        copies.append(same(ref.at[1 - ty, tc], to_core))

    def rows_wait(copies):
        arrived(copies[1:])

    def sum_start(u, lhs, lo, k):
        first = links.take(NZ)

        def step(i):
            wt = w[i, :, :, :, lo : lo + k].reshape(D // NZ, k)
            a = lhs[:, 1 - tc].reshape(2 * BLOCK, k)
            ps[u, i] = mm_nt(a, wt).astype(BF16).reshape(2, BLOCK, CH)
            links.copy(ps.at[u, i], pr.at[u, i], to_core, first + i).start()
            b = lhs[:, tc].reshape(2 * BLOCK, k)
            po[u, i] = mm_nt(b, wt).reshape(2, BLOCK, CH)

        loop(NZ, step)
        links.open += [links.copy(ps.at[u, i], pr.at[u, i], to_core, first + i) for i in range(NZ)]
        return first

    def sum_cross(u, first):
        second = links.take(NZ)

        def step(i):
            links.copy(ps.at[u, i], pr.at[u, i], to_core, first + i).wait_recv()
            other = po[u, i, 1 - ty] + pr[u, i, 1 - ty].astype(F32)
            qs[u, i] = other.astype(BF16)
            links.copy(qs.at[u, i], qr.at[u, i], to_far, second + i).start()
            po[u, i, ty] = po[u, i, ty] + pr[u, i, ty].astype(F32)

        loop(NZ, step)
        links.open += [links.copy(qs.at[u, i], qr.at[u, i], to_far, second + i) for i in range(NZ)]
        return second

    def sum_wait(u, second):
        for i in range(NZ):
            links.copy(qs.at[u, i], qr.at[u, i], to_far, second + i).wait_recv()

    def sum_rows(u, lo, n):
        return jnp.concatenate(
            [po[u, i, ty, pl.ds(lo, n), :] + qr[u, i, pl.ds(lo, n), :].astype(F32) for i in range(NZ)],
            axis=1,
        )

    def add_to(dst, src):
        dst[...] = (dst[...].astype(F32) + src[...].astype(F32)).astype(BF16)

    def g2a(p):
        c = cols(p)
        return [
            links.push(g.at[zo, 0, :, lo_half, c], r2s1.at[0, 0, :, :, c], to_zm),
            links.push(g.at[zo, 1, :, lo_half, c], r2s1.at[0, 1, :, :, c], to_zp),
            links.push(g.at[:, 0, xo, hi_half, c], r2s1.at[1, 0, :, :, c], to_xm),
            links.push(g.at[:, 1, xo, hi_half, c], r2s1.at[1, 1, :, :, c], to_xp),
        ]

    def g2b(p, copies):
        c = cols(p)
        out = []
        for k, (y, zz, to) in enumerate(((0, zm, to_zm), (1, zp, to_zp))):
            copies[k].wait_recv()
            loop(4, lambda i: add_to(g.at[zz, y, i, lo_half, c], r2s1.at[0, y, i, :, c]))
            out.append(links.push(g.at[zz, :, :, lo_half, c], r2s2z.at[y, :, :, :, c], to))
        for k, (y, xx, to) in enumerate(((0, xm, to_xm), (1, xp, to_xp))):
            copies[2 + k].wait_recv()
            loop(4, lambda i: add_to(g.at[i, y, xx, hi_half, c], r2s1.at[1, y, i, :, c]))
            out.append(links.push(g.at[:, :, xx, hi_half, c], r2s2x.at[y, :, :, :, c], to))
        return out

    def add_two(dst, a, b):
        total = dst[...].astype(F32) + a[...].astype(F32) + b[...].astype(F32)
        dst[...] = total.astype(BF16)

    def g1a(p, copies):
        c = cols(p)
        arrived(copies[:2])
        loop(
            8,
            lambda i: add_two(
                g.at[z, i // 4, i % 4, lo_half, c],
                r2s2z.at[0, i // 4, i % 4, :, c],
                r2s2z.at[1, i // 4, i % 4, :, c],
            ),
        )
        out = [
            links.push(g.at[z, 0, xo, lo_half, c], r1s1.at[0, 0, :, c], to_xm),
            links.push(g.at[z, 1, xo, lo_half, c], r1s1.at[0, 1, :, c], to_xp),
        ]
        arrived(copies[2:])
        loop(
            8,
            lambda i: add_two(
                g.at[i // 2, i % 2, x, hi_half, c],
                r2s2x.at[0, i // 2, i % 2, :, c],
                r2s2x.at[1, i // 2, i % 2, :, c],
            ),
        )
        return out + [
            links.push(g.at[zo, 0, x, hi_half, c], r1s1.at[1, 0, :, c], to_zm),
            links.push(g.at[zo, 1, x, hi_half, c], r1s1.at[1, 1, :, c], to_zp),
        ]

    def g1b(p, copies):
        c = cols(p)
        out = []
        for k, (y, xx, to) in enumerate(((0, xm, to_xm), (1, xp, to_xp))):
            copies[k].wait_recv()
            add_to(g.at[z, y, xx, lo_half, c], r1s1.at[0, y, :, c])
            out.append(links.push(g.at[z, :, xx, lo_half, c], r1s2.at[0, y, :, :, c], to))
        for k, (y, zz, to) in enumerate(((0, zm, to_zm), (1, zp, to_zp))):
            copies[2 + k].wait_recv()
            add_to(g.at[zz, y, x, hi_half, c], r1s1.at[1, y, :, c])
            out.append(links.push(g.at[zz, :, x, hi_half, c], r1s2.at[1, y, :, :, c], to))
        return out

    def gy(p, copies):
        c = cols(p)
        arrived(copies)
        for h, rows in enumerate((lo_half, hi_half)):
            loop(
                2,
                lambda y: add_two(
                    g.at[z, y, x, rows, c], r1s2.at[h, 0, y, :, c], r1s2.at[h, 1, y, :, c]
                ),
            )
        return links.push(g.at[z, 1 - yh, x, :, c], ry.at[:, c], to_y)

    def update(k, where, grad, rate):
        ref = state[k]
        found = adam_step(ref[(0, *where)], grad, ref[(1, *where)], ref[(2, *where)], rate)
        for j, value in enumerate(found):
            ref[((1, 2, 0)[j], *where)] = value

    def put(k):
        for j in range(3):
            store(state[k].at[(1, 2, 0)[j]], state_out[3 * k + j])

    def total(lo, n):
        return g[z, yh, x, :, lo : lo + n].astype(F32) + ry[:, lo : lo + n].astype(F32)

    def gend(p, copy):
        copy.wait_recv()
        if p == 0:
            for k in (1, 2):
                for j in (1, 2):
                    loads[k, j].wait()
            for j in range(3):
                update(1, (j,), total(j * CH, CH), RATE_PROJ)
            update(2, (), total(OUT_AT, CH), RATE_PROJ)
            put(1)
            put(2)
        elif p < 3:
            if p == 1:
                for j in (1, 2):
                    loads[3, j].wait()
            first, n = GU_PARTS[p - 1]
            for i in range(first, first + n):
                for j in range(2):
                    where = (j, slice(None), slice(i * TILE, (i + 1) * TILE))
                    update(3, where, total(GU_AT + (2 * i + j) * TILE, TILE), RATE_PROJ)
            if p == 2:
                put(3)
        else:
            for j in (1, 2):
                loads[4, j].wait()
            update(4, (), total(DOWN_AT, HID), RATE_DOWN)
            put(4)

    tensor_peers = (to_core, to_far, to_across)
    x_peers = (to_xp, to_xo, to_xm)
    z_peers = (to_zp, to_zo, to_zm)

    def tile_send(src, slots, first, to_all):
        return [links.push(src, slots.at[first + i], to) for i, to in enumerate(to_all)]

    def tile_sum(own, slots, first, copies):
        arrived(copies)
        return own + slots[first] + slots[first + 1] + slots[first + 2]

    s_t = tile_send(st.at[0], sr, 0, tensor_peers)
    ya = wy(0)
    tok_c = rows_start(tok)
    loads[3, 0].wait()
    for i in range(TILES):
        for j in range(2):
            lo = GU_AT + (2 * i + j) * TILE
            w[z, yh, x, :, lo : lo + TILE] = state_gu[0, j, :, i * TILE : (i + 1) * TILE].astype(BF16)
    yb = wy(1)
    ye = wy(2)
    loads[4, 0].wait()
    w[z, yh, x, :, DOWN_AT:WIDE] = state_down[0].astype(BF16)
    yc = wy(3)
    st[1] = tile_sum(st[0], sr, 0, s_t)
    s_x = tile_send(st.at[1], sr, 3, x_peers)
    ya.wait_recv()
    a1 = w1a(0)
    sm[z, yh] = tile_sum(st[1], sr, 3, s_x)
    s_y = same(sm.at[z, yh], to_y)
    arrived(a1)
    a1 = w1b(0)
    yb.wait_recv()
    b1 = w1a(1)
    s_y.wait_recv()
    s_z = [same(sm.at[z], to) for to in z_peers]
    arrived(a1)
    a2 = w2a(0)
    rows_relay(tok, tok_c)
    ye.wait_recv()
    e1 = w1a(2)
    arrived(b1)
    b1 = w1b(1)
    yc.wait_recv()
    c1 = w1a(3)
    arrived(s_z)
    for k in range(8):
        sml[:, k * TILE : (k + 1) * TILE] = sm[k // 2, k % 2]
    rows_wait(tok_c)

    def norm_in(i):
        a, b, r = i // 8, (i // 4) % 2, (i % 4) * 32
        v = tok[a, b, pl.ds(r, 32), :].astype(F32)
        inv = lax.rsqrt(jnp.mean(v * v, axis=1, keepdims=True) + NORM_EPSILON)
        one[a, b, pl.ds(r, 32), :] = (v * inv * sml[0:1, :]).astype(BF16)
        invs[a, b, pl.ds(r, 32), :] = jnp.broadcast_to(inv, (32, TILE))

    loop(16, norm_in)
    arrived(e1)
    e1 = w1b(2)
    arrived(b1)
    arrived(a2)
    a2 = w2b(0)
    b2 = w2a(1)
    arrived(c1)
    c1 = w1b(3)
    loads["cot"].wait()
    my_row = lax.broadcasted_iota(jnp.int32, (32, D), 0) + t * BLOCK

    def mask_rows(i):
        v = cot[ty, tc, pl.ds(i * 32, 32), :].astype(F32)
        cot[ty, tc, pl.ds(i * 32, 32), :] = jnp.where(my_row + i * 32 < run, v, 0.0).astype(BF16)

    loop(4, mask_rows)
    cot_c = rows_start(cot)
    arrived(a2)

    def proj(j):
        pj[j] = mm(one[...].reshape(ROWS, D), w[:, :, :, :, at_lane(j, CH)].reshape(D, CH))

    loop(3, proj)

    def taps(k, lanes):
        return sml[2 + k : 3 + k, lanes]

    for q in range(2):
        lanes = slice(q * TILE, (q + 1) * TILE)
        own = at_lane(t * 2 + q, TILE)
        mixed = pj[0, :, lanes] * pj[2, :, lanes]
        before_one = pltpu.roll(mixed, 1, 0) * masks[0]
        before_two = pltpu.roll(mixed, 2, 0) * masks[1]
        v = taps(0, own) * mixed + taps(1, own) * before_one + taps(2, own) * before_two
        conv[:, lanes] = v
        gated[:, :, :, lanes] = (pj[1, :, lanes] * v).astype(BF16).reshape(2, 2, BLOCK, TILE)

    m_first = sum_start(0, gated, OUT_AT, CH)
    arrived(b2)
    b2 = w2b(1)
    arrived(e1)
    e2 = w2a(2)
    m_second = sum_cross(0, m_first)
    sum_wait(0, m_second)

    def norm_mid(i):
        r = i * 32
        v = tok[ty, tc, pl.ds(r, 32), :].astype(F32) + sum_rows(0, r, 32)
        mid[pl.ds(r, 32), :] = v
        inv = lax.rsqrt(jnp.mean(v * v, axis=1, keepdims=True) + NORM_EPSILON)
        two[ty, tc, pl.ds(r, 32), :] = (v * inv * sml[1:2, :]).astype(BF16)

    loop(4, norm_mid)
    two_c = rows_start(two)
    rows_relay(cot, cot_c)
    arrived(e2)
    e2 = w2b(2)
    arrived(c1)
    c2 = w2a(3)
    rows_relay(two, two_c)
    rows_wait(two_c)
    arrived(b2)

    def gate_up(i):
        lanes = pl.ds(pl.multiple_of(GU_AT + i * CH, CH), CH)
        v = mm(two[...].reshape(ROWS, D), w[:, :, :, :, lanes].reshape(D, CH))
        gate, up = v[:, :TILE], v[:, TILE:]
        s = jax.nn.sigmoid(gate)
        act = gate * s
        hid[:, :, :, at_lane(i, TILE)] = (act * up).astype(BF16).reshape(2, 2, BLOCK, TILE)
        gu[i, :, :TILE] = up * s * (1.0 + gate * (1.0 - s))
        gu[i, :, TILE:] = act

    loop(FIRST, gate_up)
    arrived(e2)
    loop(TILES - FIRST, lambda i: gate_up(i + FIRST))
    arrived(c2)
    c2 = w2b(3)
    rows_wait(cot_c)

    def wide(v):
        return v.reshape(NY, NX, SHARD, v.shape[1])

    def down_grad(i):
        a = cot[:, :, :, at_lane(i, CH)].reshape(ROWS, CH).T
        g[i, :, :, :, DOWN_AT:WIDE] = wide(mm(a, hid[...].reshape(ROWS, HID)).astype(BF16))

    loop(NZ, down_grad)
    gc_ = g2a(3)
    arrived(c2)

    def back_tile(k, gh):
        v = gu[k]
        gg[:, :, :, at_lane(2 * k, TILE)] = (gh * v[:, :TILE]).astype(BF16).reshape(2, 2, BLOCK, TILE)
        gg[:, :, :, at_lane(2 * k + 1, TILE)] = (
            (gh * v[:, TILE:]).astype(BF16).reshape(2, 2, BLOCK, TILE)
        )

    def grad_hidden(i):
        lanes = pl.ds(pl.multiple_of(DOWN_AT + i * CH, TILE), CH)
        v = mm(cot[...].reshape(ROWS, D), w[:, :, :, :, lanes].reshape(D, CH))
        back_tile(2 * i, v[:, :TILE])
        back_tile(2 * i + 1, v[:, TILE:])

    def gate_up_grad(p):
        first, n = GU_PARTS[p - 1]

        def step(i):
            a = two[:, :, :, at_lane(i, CH)].reshape(ROWS, CH).T
            b = gg[:, :, :, first * CH : (first + n) * CH].reshape(ROWS, n * CH)
            lo = GU_AT + first * CH
            g[i, :, :, :, lo : lo + n * CH] = wide(mm(a, b).astype(BF16))

        loop(NZ, step)

    loop(TILES // 2, grad_hidden)
    back_tile(
        TILES - 1,
        mm(cot[...].reshape(ROWS, D), w[:, :, :, :, WIDE - TILE : WIDE].reshape(D, TILE)),
    )
    gc_ = g2b(3, gc_)
    gate_up_grad(1)
    gb_ = g2a(1)
    n_first = sum_start(1, gg, GU_AT, 2 * HID)
    gate_up_grad(2)
    ge_ = g2a(2)
    n_second = sum_cross(1, n_first)
    gc_ = g1a(3, gc_)
    gb_ = g2b(1, gb_)
    sum_wait(1, n_second)
    gacc[...] = jnp.zeros_like(gacc)

    def norm_two_back(i):
        r = i * 32
        gn = sum_rows(1, r, 32)
        v = mid[pl.ds(r, 32), :]
        inv = lax.rsqrt(jnp.mean(v * v, axis=1, keepdims=True) + NORM_EPSILON)
        unit = v * inv
        gacc[1:2, :] += jnp.sum(gn * unit, axis=0, keepdims=True)
        scaled = gn * sml[1:2, :]
        inner = jnp.mean(scaled * unit, axis=1, keepdims=True)
        out = cot[ty, tc, pl.ds(r, 32), :].astype(F32) + inv * (scaled - unit * inner)
        gmid[pl.ds(r, 32), :] = out
        rmid[ty, tc, pl.ds(r, 32), :] = out.astype(BF16)

    loop(4, norm_two_back)
    mid_c = rows_start(rmid)
    o_first = sum_start(2, hid, DOWN_AT, HID)
    ge_ = g2b(2, ge_)
    gc_ = g1b(3, gc_)
    rows_relay(rmid, mid_c)
    o_second = sum_cross(2, o_first)
    rows_wait(mid_c)

    pg = mm(rmid[...].reshape(ROWS, D), w[:, :, :, :, OUT_AT : OUT_AT + CH].reshape(D, CH))
    for q in range(2):
        lanes = slice(q * TILE, (q + 1) * TILE)
        own = at_lane(t * 2 + q, TILE)
        gate_b, gate_c, values = pj[0, :, lanes], pj[1, :, lanes], pj[2, :, lanes]
        mixed = gate_b * values
        gv = pg[:, lanes]
        grad_c = gv * conv[:, lanes]
        grad_conv = gv * gate_c
        one_grad, two_grad = grad_conv * masks[0], grad_conv * masks[1]
        gacc[2:3, own] = jnp.sum(grad_conv * mixed, axis=0, keepdims=True)
        gacc[3:4, own] = jnp.sum(one_grad * pltpu.roll(mixed, 1, 0), axis=0, keepdims=True)
        gacc[4:5, own] = jnp.sum(two_grad * pltpu.roll(mixed, 2, 0), axis=0, keepdims=True)
        grad_mixed = (
            taps(0, own) * grad_conv
            + taps(1, own) * pltpu.roll(one_grad, ROWS - 1, 0)
            + taps(2, own) * pltpu.roll(two_grad, ROWS - 2, 0)
        )
        for j, v in enumerate((grad_mixed * values, grad_c, grad_mixed * gate_b)):
            lo = j * CH + q * TILE
            gp[:, :, :, lo : lo + TILE] = v.astype(BF16).reshape(2, 2, BLOCK, TILE)

    i_first = sum_start(3, gp, 0, 3 * CH)

    def mix_grad(i):
        a = one[:, :, :, at_lane(i, CH)].reshape(ROWS, CH).T
        g[i, :, :, :, :OUT_AT] = wide(mm(a, gp[...].reshape(ROWS, 3 * CH)).astype(BF16))
        b = rmid[:, :, :, at_lane(i, CH)].reshape(ROWS, CH).T
        g[i, :, :, :, OUT_AT:GU_AT] = wide(mm(b, gated[...].reshape(ROWS, CH)).astype(BF16))

    loop(NZ, mix_grad)
    ga_ = g2a(0)

    def gain_one(i):
        lanes = at_lane(i, CH)
        out = jnp.zeros((1, CH), F32)
        for c, terms in ((1 - tc, ps), (tc, po)):
            for a in range(2):
                unit = tok[a, c, :, lanes].astype(F32) * jnp.tile(invs[a, c], (1, 2))
                out += jnp.sum(terms[3, i, a].astype(F32) * unit, axis=0, keepdims=True)
        gacc[0:1, lanes] = out

    loop(NZ, gain_one)
    for k in range(8):
        sgr[k // 2, k % 2] = gacc[:, k * TILE : (k + 1) * TILE]
    u_z = [
        links.push(sgr.at[zz], gr.at[i], to)
        for i, (zz, to) in enumerate(((zp, to_zp), (zo, to_zo), (zm, to_zm)))
    ]
    i_second = sum_cross(3, i_first)
    gb_ = g1a(1, gb_)
    gc_ = gy(3, gc_)
    arrived(u_z)
    sgr[z] = sgr[z] + gr[0] + gr[1] + gr[2]
    u_y = links.push(sgr.at[z, 1 - yh], gc.at[0], to_y)
    ge_ = g1a(2, ge_)
    ga_ = g2b(0, ga_)
    gb_ = g1b(1, gb_)
    u_y.wait_recv()
    gc[1] = sgr[z, yh] + gc[0]
    u_x = tile_send(gc.at[1], gc, 2, x_peers)
    sum_wait(2, o_second)

    def out_rows(i):
        r = i * 32
        bo[pl.ds(r, 32), :] = (mid[pl.ds(r, 32), :] + sum_rows(2, r, 32)).astype(BF16)

    loop(4, out_rows)
    store(bo, bo_out)
    ge_ = g1b(2, ge_)
    gb_ = gy(1, gb_)
    gend(3, gc_)
    gc[5] = tile_sum(gc[1], gc, 2, u_x)
    u_t = tile_send(gc.at[5], gc, 6, tensor_peers)
    sum_wait(3, i_second)

    def norm_one_back(i):
        r = i * 32
        gn = sum_rows(3, r, 32)
        unit = tok[ty, tc, pl.ds(r, 32), :].astype(F32)
        inv = lax.rsqrt(jnp.mean(unit * unit, axis=1, keepdims=True) + NORM_EPSILON)
        unit = unit * inv
        scaled = gn * sml[0:1, :]
        inner = jnp.mean(scaled * unit, axis=1, keepdims=True)
        tg[pl.ds(r, 32), :] = gmid[pl.ds(r, 32), :] + inv * (scaled - unit * inner)

    loop(4, norm_one_back)
    store(tg, tg_out)
    ge_ = gy(2, ge_)
    gend(1, gb_)
    ga_ = g1a(0, ga_)
    gc[9] = pltpu.roll(tile_sum(gc[5], gc, 6, u_t), TILE - place, 1)
    for j in (1, 2):
        loads[0, j].wait()
    update(0, (), gc[9, 0:5, 0:8], RATE_SMALL)
    put(0)
    gend(2, ge_)
    ga_ = g1b(0, ga_)
    ga_ = gy(0, ga_)
    gend(0, ga_)
    for c in links.open:
        c.wait_send()
    for c in stores:
        c.wait()


N_COPIES = 220


def train_call(lengths, tokens, cotangent, *state):
    anywhere = pl.BlockSpec(memory_space=pltpu.HBM)
    rows = (2, 2, BLOCK)
    weights = state[:5]
    out_shape = [jax.ShapeDtypeStruct((BLOCK, D), BF16), jax.ShapeDtypeStruct((BLOCK, D), F32)]
    for v in weights:
        out_shape += [jax.ShapeDtypeStruct(v.shape, F32)] * 3
    return pl.pallas_call(
        train_kernel,
        out_shape=out_shape,
        in_specs=[pl.BlockSpec(memory_space=pltpu.SMEM)] + [anywhere] * 17,
        out_specs=[anywhere] * 17,
        scratch_shapes=[pltpu.VMEM((3,) + v.shape, F32) for v in weights]
        + [
            pltpu.VMEM((BLOCK, D), BF16),
            pltpu.VMEM((BLOCK, D), F32),
            pltpu.SemaphoreType.DMA((40,)),
            pltpu.VMEM((NZ, NY, NX, SHARD, WIDE), BF16),
            pltpu.VMEM((NZ, NY, NX, SHARD, WIDE), BF16),
            pltpu.VMEM(rows + (D,), BF16),
            pltpu.VMEM(rows + (D,), BF16),
            pltpu.VMEM(rows + (D,), BF16),
            pltpu.VMEM(rows + (D,), BF16),
            pltpu.VMEM(rows + (D,), BF16),
            pltpu.VMEM((2, ROWS, TILE), F32),
            pltpu.VMEM((3, ROWS, CH), F32),
            pltpu.VMEM((ROWS, CH), F32),
            pltpu.VMEM(rows + (CH,), BF16),
            pltpu.VMEM(rows + (3 * CH,), BF16),
            pltpu.VMEM((TILES, ROWS, CH), F32),
            pltpu.VMEM(rows + (HID,), BF16),
            pltpu.VMEM(rows + (2 * HID,), BF16),
            pltpu.VMEM((BLOCK, D), F32),
            pltpu.VMEM((BLOCK, D), F32),
            pltpu.VMEM((8, D), F32),
            pltpu.VMEM((2, 8, TILE), F32),
            pltpu.VMEM((6, 8, TILE), F32),
            pltpu.VMEM((NZ, NY, 8, TILE), F32),
            pltpu.VMEM((NZ, NY, 8, TILE), F32),
            pltpu.VMEM((3, NY, 8, TILE), F32),
            pltpu.VMEM((10, 8, TILE), F32),
            pltpu.VMEM((8, D), F32),
            pltpu.VMEM(rows + (TILE,), F32),
            pltpu.VMEM((4, NZ, 2, BLOCK, CH), BF16),
            pltpu.VMEM((4, NZ, 2, BLOCK, CH), BF16),
            pltpu.VMEM((4, NZ, 2, BLOCK, CH), F32),
            pltpu.VMEM((4, NZ, BLOCK, CH), BF16),
            pltpu.VMEM((4, NZ, BLOCK, CH), BF16),
            pltpu.VMEM((2, 2, 4, HALF, WIDE), BF16),
            pltpu.VMEM((2, NY, NX, HALF, WIDE), BF16),
            pltpu.VMEM((2, NZ, NY, HALF, WIDE), BF16),
            pltpu.VMEM((2, 2, HALF, WIDE), BF16),
            pltpu.VMEM((2, 2, 2, HALF, WIDE), BF16),
            pltpu.VMEM((SHARD, WIDE), BF16),
            pltpu.SemaphoreType.DMA((N_COPIES,)),
            pltpu.SemaphoreType.DMA((N_COPIES,)),
        ],
        compiler_params=pltpu.CompilerParams(
            collective_id=0, has_side_effects=True, vmem_limit_bytes=63 * 1024 * 1024
        ),
        cost_estimate=pl.CostEstimate(
            flops=6 * ROWS * D * WIDE, bytes_accessed=8 * 1024 * 1024, transcendentals=ROWS * HID
        ),
    )(lengths, tokens, cotangent, *state)


def hand_over(*refs):
    n = (len(refs) - 2) // 3
    sources, targets, held = refs[:n], refs[n : 2 * n], refs[2 * n : 3 * n]
    load_sem, store_sem = refs[3 * n :]
    loads = [pltpu.make_async_copy(sources[i], held[i], load_sem.at[i]) for i in range(n)]
    stores = [pltpu.make_async_copy(held[i], targets[i], store_sem.at[i]) for i in range(n)]
    for c in loads:
        c.start()
    for i in range(n):
        loads[i].wait()
        stores[i].start()
    for c in stores:
        c.wait()


def per_device(
    tokens,
    cotangent,
    lengths,
    small,
    mix_in,
    mix_out,
    ffn_gate_up,
    ffn_down,
    small_first,
    small_second,
    in_first,
    in_second,
    out_first,
    out_second,
    gate_up_first,
    gate_up_second,
    down_first,
    down_second,
):
    found = train_call(
        lengths,
        tokens,
        cotangent,
        small,
        mix_in,
        mix_out,
        ffn_gate_up,
        ffn_down,
        small_first,
        small_second,
        in_first,
        in_second,
        out_first,
        out_second,
        gate_up_first,
        gate_up_second,
        down_first,
        down_second,
    )
    anywhere = pl.BlockSpec(memory_space=pltpu.HBM)
    n = len(found)
    return tuple(
        pl.pallas_call(
            hand_over,
            out_shape=[jax.ShapeDtypeStruct(v.shape, v.dtype) for v in found],
            in_specs=[anywhere] * n,
            out_specs=[anywhere] * n,
            scratch_shapes=[pltpu.VMEM(v.shape, v.dtype) for v in found]
            + [pltpu.SemaphoreType.DMA((n,))] * 2,
        )(*found)
    )


def solution(mesh):
    rows = P(("dp", "tensor"), None)
    small = P(None, ("dp", "tensor"))
    deep = P(None, "dp", "tensor")
    flat = P("dp", "tensor")
    in_specs = (rows, rows, P("dp", None), small, deep, flat, deep, flat)
    in_specs += (small,) * 2 + (deep,) * 2 + (flat,) * 2 + (deep,) * 2 + (flat,) * 2
    out_specs = (rows, rows) + (small,) * 3 + (deep,) * 3 + (flat,) * 3 + (deep,) * 3 + (flat,) * 3
    return jax.shard_map(
        per_device, mesh=mesh, in_specs=in_specs, out_specs=out_specs, check_vma=False
    )
```

```python
import functools

import jax
import jax.numpy as jnp
from jax import lax
from jax.experimental import pallas as pl
from jax.experimental.pallas import tpu as pltpu
from jax.sharding import PartitionSpec as P

STEP = 10
NORM_EPSILON = 1e-05
BETA_FIRST = 0.9
BETA_SECOND = 0.95
ADAM_EPSILON = 1e-08
DECAY_RATE = 0.1
RATE_PROJ = 0.1
RATE_DOWN = 0.045
RATE_SMALL = 0.6

MESH = pl.DeviceIdType.MESH
F32 = jnp.float32
BF16 = jnp.bfloat16

D = 1024
ROWS = 512
BLOCK = 128
CH = 256
HID = 1152
TILE = 128
TILES = HID // TILE
OUT_AT = 3 * CH
GU_AT = 4 * CH
DOWN_AT = GU_AT + 2 * HID
WIDE = DOWN_AT + HID
FIRST = TILES // 2
GU_PARTS = ((0, FIRST), (FIRST, TILES - FIRST))
PARTS = (
    (0, GU_AT),
    (GU_AT, FIRST * CH),
    (GU_AT + FIRST * CH, (TILES - FIRST) * CH),
    (DOWN_AT, HID),
)
NZ, NY, NX, SHARD = 4, 2, 4, 32
HALF = SHARD // 2


def mm(a, b):
    return lax.dot_general(a, b, (((1,), (0,)), ((), ())), preferred_element_type=F32)


def mm_nt(a, b):
    return lax.dot_general(a, b, (((1,), (1,)), ((), ())), preferred_element_type=F32)


def loop(n, body):
    lax.fori_loop(0, n, lambda i, carry: (body(i), carry)[1], 0)


def at_lane(i, width):
    return pl.ds(pl.multiple_of(i * width, width), width)


def adam_step(weight, grad, first, second, rate):
    first_new = BETA_FIRST * first + (1.0 - BETA_FIRST) * grad
    second_new = BETA_SECOND * second + (1.0 - BETA_SECOND) * grad * grad
    first_hat = first_new / (1.0 - BETA_FIRST**STEP)
    second_hat = second_new / (1.0 - BETA_SECOND**STEP)
    weight_new = weight - rate * (
        first_hat / (jnp.sqrt(second_hat) + ADAM_EPSILON) + DECAY_RATE * weight
    )
    return (first_new, second_new, weight_new)


class Links:
    def __init__(self, send, recv):
        self.send, self.recv, self.used, self.open = send, recv, 0, []

    def take(self, n=1):
        first = self.used
        self.used += n
        return first

    def copy(self, src, dst, to, slot):
        return pltpu.make_async_remote_copy(
            src_ref=src,
            dst_ref=dst,
            send_sem=self.send.at[slot],
            recv_sem=self.recv.at[slot],
            device_id=to,
            device_id_type=MESH,
        )

    def push(self, src, dst, to):
        c = self.copy(src, dst, to, self.take())
        c.start()
        self.open.append(c)
        return c


def arrived(copies):
    for c in copies:
        c.wait_recv()


def train_kernel(*refs):
    lens, tok_in, cot_in = refs[:3]
    state_in = refs[3:18]
    bo_out, tg_out = refs[18:20]
    state_out = refs[20:35]
    train_body(lens, tok_in, cot_in, state_in, bo_out, tg_out, state_out, *refs[35:])


def train_body(
    lens,
    tok_in,
    cot_in,
    state_in,
    bo_out,
    tg_out,
    state_out,
    state_small,
    state_in_w,
    state_out_w,
    state_gu,
    state_down,
    bo,
    tg,
    local_sem,
    w,
    g,
    tok,
    cot,
    one,
    two,
    rmid,
    masks,
    pj,
    conv,
    gated,
    gp,
    gu,
    hid,
    gg,
    mid,
    gmid,
    sml,
    st,
    sr,
    sm,
    sgr,
    gr,
    gc,
    gacc,
    invs,
    ps,
    pr,
    po,
    qs,
    qr,
    r2s1,
    r2s2z,
    r2s2x,
    r1s1,
    r1s2,
    ry,
    send_sem,
    recv_sem,
):
    dp = lax.axis_index("dp")
    t = lax.axis_index("tensor")
    z, yh, x = dp // 8, (dp // 4) % 2, dp % 4
    ty, tc = t // 2, t % 2
    zp, zm, zo = (z + 1) % 4, (z + 3) % 4, (z + 2) % 4
    xp, xm, xo = (x + 1) % 4, (x + 3) % 4, (x + 2) % 4

    def at(zz, yy, xx):
        return (zz * 8 + yy * 4 + xx, t)

    to_y = at(z, 1 - yh, x)
    to_xp, to_xm = at(z, yh, xp), at(z, yh, xm)
    to_zp, to_zm = at(zp, yh, x), at(zm, yh, x)
    to_xo, to_zo = at(z, yh, xo), at(zo, yh, x)
    to_core = (dp, ty * 2 + 1 - tc)
    to_far = (dp, (1 - ty) * 2 + tc)
    to_across = (dp, (1 - ty) * 2 + 1 - tc)
    tensor_peers = (to_core, to_far, to_across)
    x_peers = (to_xp, to_xo, to_xm)
    z_peers = (to_zp, to_zo, to_zm)
    links = Links(send_sem, recv_sem)

    barrier = pltpu.get_barrier_semaphore()
    peers = (to_y, to_xp, to_xm, to_xo, to_zp, to_zm, to_zo, to_core, to_far, to_across)
    for to in peers:
        pl.semaphore_signal(barrier, inc=1, device_id=to, device_id_type=MESH)

    state = (state_small, state_in_w, state_out_w, state_gu, state_down)
    n_local = 0
    loads = {}
    for key, src, dst in (
        [((k, 0), state_in[k], state[k].at[0]) for k in range(5)]
        + [("tok", tok_in, tok.at[ty, tc]), ("cot", cot_in, cot.at[ty, tc])]
        + [((k, j), state_in[3 + 2 * k + j + 1], state[k].at[j]) for k in range(5) for j in (1, 2)]
    ):
        loads[key] = pltpu.make_async_copy(src, dst, local_sem.at[n_local])
        loads[key].start()
        n_local += 1
    stores = []

    def store(src, dst):
        c = pltpu.make_async_copy(src, dst, local_sem.at[n_local + len(stores)])
        c.start()
        stores.append(c)

    row = lax.broadcasted_iota(jnp.int32, (ROWS, TILE), 0)
    start = jnp.zeros((ROWS, TILE), jnp.int32)
    run = jnp.int32(0)
    for k in range(lens.shape[1]):
        run = run + lens[0, k]
        start = jnp.where(row >= run, run, start)
    dist = row - start
    masks[0] = jnp.where(dist >= 1, 1.0, 0.0)
    masks[1] = jnp.where(dist >= 2, 1.0, 0.0)

    place = ((dp % 4) * 4 + t) * 8
    st[0] = jnp.zeros((8, TILE), F32)
    loads[0, 0].wait()
    st[0, 0:5, 0:8] = state_small[0]
    st[0] = pltpu.roll(st[0], place, 1)
    loads[1, 0].wait()
    for j in range(3):
        w[z, yh, x, :, j * CH : (j + 1) * CH] = state_in_w[0, j].astype(BF16)
    loads[2, 0].wait()
    w[z, yh, x, :, OUT_AT : OUT_AT + CH] = state_out_w[0].astype(BF16)
    loads[3, 0].wait()
    for i in range(TILES):
        for j in range(2):
            lo = GU_AT + (2 * i + j) * TILE
            w[z, yh, x, :, lo : lo + TILE] = state_gu[0, j, :, i * TILE : (i + 1) * TILE].astype(BF16)
    loads[4, 0].wait()
    w[z, yh, x, :, DOWN_AT:WIDE] = state_down[0].astype(BF16)
    loads["tok"].wait()
    pl.semaphore_wait(barrier, len(peers))

    lo_half, hi_half = pl.ds(0, HALF), pl.ds(HALF, HALF)

    def cols(part):
        return pl.ds(PARTS[part][0], PARTS[part][1])

    def same(ref, to):
        return links.push(ref, ref, to)

    def wy(p):
        return same(w.at[z, yh, x, :, cols(p)], to_y)

    def w1a(p):
        a, b = w.at[z, :, x, lo_half, cols(p)], w.at[z, :, x, hi_half, cols(p)]
        return [same(a, to_xp), same(a, to_xm), same(b, to_zp), same(b, to_zm)]

    def w1_all(p):
        a, b = w.at[z, :, x, lo_half, cols(p)], w.at[z, :, x, hi_half, cols(p)]
        return [same(a, to) for to in x_peers] + [same(b, to) for to in z_peers]

    def w1b(p):
        return [
            same(w.at[z, 0, xm, lo_half, cols(p)], to_xp),
            same(w.at[z, 1, xp, lo_half, cols(p)], to_xm),
            same(w.at[zm, 0, x, hi_half, cols(p)], to_zp),
            same(w.at[zp, 1, x, hi_half, cols(p)], to_zm),
        ]

    def w2a(p):
        a, b = w.at[z, :, :, lo_half, cols(p)], w.at[:, :, x, hi_half, cols(p)]
        return [same(a, to_zp), same(a, to_zm), same(b, to_xp), same(b, to_xm)]

    def w2b(p):
        return [
            same(w.at[zm, 0, :, lo_half, cols(p)], to_zp),
            same(w.at[zp, 1, :, lo_half, cols(p)], to_zm),
            same(w.at[:, 0, xm, hi_half, cols(p)], to_xp),
            same(w.at[:, 1, xp, hi_half, cols(p)], to_xm),
        ]

    def rows_start(ref):
        mine = ref.at[ty, tc]
        return [same(mine, to_far), same(mine, to_core)]

    def rows_relay(ref, copies):
        copies[0].wait_recv()
        copies.append(same(ref.at[1 - ty, tc], to_core))

    def rows_wait(copies):
        arrived(copies[1:])

    def piece(i):
        return pl.ds(i * (BLOCK // NZ), BLOCK // NZ)

    class Pieces:
        def __init__(self, ref):
            self.ref, self.first = ref, links.take(3 * NZ)

        def part(self, kind, i):
            mine = self.ref.at[(1 - ty) if kind == 2 else ty, tc, piece(i)]
            to = to_far if kind == 0 else to_core
            return links.copy(mine, mine, to, self.first + kind * NZ + i)

        def push(self, i):
            self.part(0, i).start()
            self.part(1, i).start()

        def relay(self):
            def step(i):
                self.part(0, i).wait_recv()
                self.part(2, i).start()

            loop(NZ, step)

        def wait(self):
            for i in range(NZ):
                self.part(1, i).wait_recv()
                self.part(2, i).wait_recv()
            links.open += [self.part(kind, i) for kind in range(3) for i in range(NZ)]

    def sum_start(u, lhs, lo, k):
        first, second = links.take(NZ), links.take(NZ)

        def near(i):
            return links.copy(ps.at[u, i], pr.at[u, i], to_core, first + i)

        def far(i):
            return links.copy(qs.at[u, i], qr.at[u, i], to_far, second + i)

        def step(i):
            wt = w[i, :, :, :, lo : lo + k].reshape(D // NZ, k)
            a = lhs[:, 1 - tc].reshape(2 * BLOCK, k)
            ps[u, i] = mm_nt(a, wt).astype(BF16).reshape(2, BLOCK, CH)
            near(i).start()
            b = lhs[:, tc].reshape(2 * BLOCK, k)
            po[u, i] = mm_nt(b, wt).reshape(2, BLOCK, CH)

        def cross(i):
            near(i).wait_recv()
            other = po[u, i, 1 - ty] + pr[u, i, 1 - ty].astype(F32)
            qs[u, i] = other.astype(BF16)
            far(i).start()

        def both(i):
            step(i + 1)
            cross(i)

        step(0)
        loop(NZ - 1, both)
        cross(NZ - 1)
        links.open += [near(i) for i in range(NZ)] + [far(i) for i in range(NZ)]
        return second

    def sum_wait(u, second):
        for i in range(NZ):
            links.copy(qs.at[u, i], qr.at[u, i], to_far, second + i).wait_recv()

    def sum_rows(u, lo, n):
        return jnp.concatenate(
            [
                po[u, i, ty, pl.ds(lo, n), :]
                + pr[u, i, ty, pl.ds(lo, n), :].astype(F32)
                + qr[u, i, pl.ds(lo, n), :].astype(F32)
                for i in range(NZ)
            ],
            axis=1,
        )

    def add_to(dst, src):
        dst[...] = (dst[...].astype(F32) + src[...].astype(F32)).astype(BF16)

    def g2a(p):
        c = cols(p)
        return [
            links.push(g.at[zo, 0, :, lo_half, c], r2s1.at[0, 0, :, :, c], to_zm),
            links.push(g.at[zo, 1, :, lo_half, c], r2s1.at[0, 1, :, :, c], to_zp),
            links.push(g.at[:, 0, xo, hi_half, c], r2s1.at[1, 0, :, :, c], to_xm),
            links.push(g.at[:, 1, xo, hi_half, c], r2s1.at[1, 1, :, :, c], to_xp),
        ]

    def g2b(p, copies):
        c = cols(p)
        out = []
        for k, (y, zz, to) in enumerate(((0, zm, to_zm), (1, zp, to_zp))):
            copies[k].wait_recv()
            loop(4, lambda i: add_to(g.at[zz, y, i, lo_half, c], r2s1.at[0, y, i, :, c]))
            out.append(links.push(g.at[zz, :, :, lo_half, c], r2s2z.at[y, :, :, :, c], to))
        for k, (y, xx, to) in enumerate(((0, xm, to_xm), (1, xp, to_xp))):
            copies[2 + k].wait_recv()
            loop(4, lambda i: add_to(g.at[i, y, xx, hi_half, c], r2s1.at[1, y, i, :, c]))
            out.append(links.push(g.at[:, :, xx, hi_half, c], r2s2x.at[y, :, :, :, c], to))
        return out

    def add_two(dst, a, b):
        total = dst[...].astype(F32) + a[...].astype(F32) + b[...].astype(F32)
        dst[...] = total.astype(BF16)

    def g1a(p, copies):
        c = cols(p)
        arrived(copies[:2])
        loop(
            8,
            lambda i: add_two(
                g.at[z, i // 4, i % 4, lo_half, c],
                r2s2z.at[0, i // 4, i % 4, :, c],
                r2s2z.at[1, i // 4, i % 4, :, c],
            ),
        )
        out = [
            links.push(g.at[z, 0, xo, lo_half, c], r1s1.at[0, 0, :, c], to_xm),
            links.push(g.at[z, 1, xo, lo_half, c], r1s1.at[0, 1, :, c], to_xp),
        ]
        arrived(copies[2:])
        loop(
            8,
            lambda i: add_two(
                g.at[i // 2, i % 2, x, hi_half, c],
                r2s2x.at[0, i // 2, i % 2, :, c],
                r2s2x.at[1, i // 2, i % 2, :, c],
            ),
        )
        return out + [
            links.push(g.at[zo, 0, x, hi_half, c], r1s1.at[1, 0, :, c], to_zm),
            links.push(g.at[zo, 1, x, hi_half, c], r1s1.at[1, 1, :, c], to_zp),
        ]

    def sum_second(p, copies):
        c = cols(p)
        arrived(copies)
        loop(
            8,
            lambda i: add_two(
                g.at[z, i // 4, i % 4, lo_half, c],
                r2s2z.at[0, i // 4, i % 4, :, c],
                r2s2z.at[1, i // 4, i % 4, :, c],
            ),
        )
        loop(
            8,
            lambda i: add_two(
                g.at[i // 2, i % 2, x, hi_half, c],
                r2s2x.at[0, i // 2, i % 2, :, c],
                r2s2x.at[1, i // 2, i % 2, :, c],
            ),
        )

    def g1_all(p, copies):
        c = cols(p)
        sum_second(p, copies)
        out = []
        for i, (xx, to) in enumerate(((xp, to_xp), (xo, to_xo), (xm, to_xm))):
            out.append(links.push(g.at[z, :, xx, lo_half, c], r1s2.at[0, i, :, :, c], to))
        for i, (zz, to) in enumerate(((zp, to_zp), (zo, to_zo), (zm, to_zm))):
            out.append(links.push(g.at[zz, :, x, hi_half, c], r1s2.at[1, i, :, :, c], to))
        return out

    def gy_all(p, copies):
        c = cols(p)
        arrived(copies)
        for h, rows in enumerate((lo_half, hi_half)):
            for y in range(2):
                total = g[z, y, x, rows, c].astype(F32)
                for i in range(3):
                    total = total + r1s2[h, i, y, :, c].astype(F32)
                g[z, y, x, rows, c] = total.astype(BF16)
        return links.push(g.at[z, 1 - yh, x, :, c], ry.at[:, c], to_y)

    def g1b(p, copies):
        c = cols(p)
        out = []
        for k, (y, xx, to) in enumerate(((0, xm, to_xm), (1, xp, to_xp))):
            copies[k].wait_recv()
            add_to(g.at[z, y, xx, lo_half, c], r1s1.at[0, y, :, c])
            out.append(links.push(g.at[z, :, xx, lo_half, c], r1s2.at[0, y, :, :, c], to))
        for k, (y, zz, to) in enumerate(((0, zm, to_zm), (1, zp, to_zp))):
            copies[2 + k].wait_recv()
            add_to(g.at[zz, y, x, hi_half, c], r1s1.at[1, y, :, c])
            out.append(links.push(g.at[zz, :, x, hi_half, c], r1s2.at[1, y, :, :, c], to))
        return out

    def gy(p, copies):
        c = cols(p)
        arrived(copies)
        for h, rows in enumerate((lo_half, hi_half)):
            loop(
                2,
                lambda y: add_two(
                    g.at[z, y, x, rows, c], r1s2.at[h, 0, y, :, c], r1s2.at[h, 1, y, :, c]
                ),
            )
        return links.push(g.at[z, 1 - yh, x, :, c], ry.at[:, c], to_y)

    def update(k, where, grad, rate):
        ref = state[k]
        found = adam_step(ref[(0, *where)], grad, ref[(1, *where)], ref[(2, *where)], rate)
        for j, value in enumerate(found):
            ref[((1, 2, 0)[j], *where)] = value

    def put(k):
        for j in range(3):
            store(state[k].at[(1, 2, 0)[j]], state_out[3 * k + j])

    def total(lo, n):
        return g[z, yh, x, :, lo : lo + n].astype(F32) + ry[:, lo : lo + n].astype(F32)

    def gend(p, copy):
        copy.wait_recv()
        if p == 0:
            for k in (1, 2):
                for j in (1, 2):
                    loads[k, j].wait()
            for j in range(3):
                update(1, (j,), total(j * CH, CH), RATE_PROJ)
            update(2, (), total(OUT_AT, CH), RATE_PROJ)
            put(1)
            put(2)
        elif p < 3:
            if p == 1:
                for j in (1, 2):
                    loads[3, j].wait()
            first, n = GU_PARTS[p - 1]
            for i in range(first, first + n):
                for j in range(2):
                    where = (j, slice(None), slice(i * TILE, (i + 1) * TILE))
                    update(3, where, total(GU_AT + (2 * i + j) * TILE, TILE), RATE_PROJ)
            if p == 2:
                put(3)
        else:
            for j in (1, 2):
                loads[4, j].wait()
            update(4, (), total(DOWN_AT, HID), RATE_DOWN)
            put(4)


    def tile_send(src, slots, first, to_all):
        return [links.push(src, slots.at[first + i], to) for i, to in enumerate(to_all)]

    def tile_sum(own, slots, first, copies):
        arrived(copies)
        return own + slots[first] + slots[first + 1] + slots[first + 2]

    s_t = tile_send(st.at[0], sr, 0, tensor_peers)
    ya = wy(0)
    yb = wy(1)
    ye = wy(2)
    yc = wy(3)
    tok_c = rows_start(tok)
    st[1] = tile_sum(st[0], sr, 0, s_t)
    s_x = tile_send(st.at[1], sr, 3, x_peers)
    ya.wait_recv()
    a1 = w1_all(0)
    sm[z, yh] = tile_sum(st[1], sr, 3, s_x)
    s_y = same(sm.at[z, yh], to_y)
    yb.wait_recv()
    b1 = w1a(1)
    arrived(a1)
    a2 = w2a(0)
    s_y.wait_recv()
    s_z = [same(sm.at[z], to) for to in z_peers]
    ye.wait_recv()
    e1 = w1a(2)
    arrived(b1)
    b1 = w1b(1)
    yc.wait_recv()
    c1 = w1a(3)
    arrived(e1)
    e1 = w1b(2)
    rows_relay(tok, tok_c)
    arrived(s_z)
    for k in range(8):
        sml[:, k * TILE : (k + 1) * TILE] = sm[k // 2, k % 2]
    arrived(b1)
    arrived(a2)
    a2 = w2b(0)
    b2 = w2a(1)
    rows_wait(tok_c)

    def norm_in(i):
        a, b, r = i // 8, (i // 4) % 2, (i % 4) * 32
        v = tok[a, b, pl.ds(r, 32), :].astype(F32)
        inv = lax.rsqrt(jnp.mean(v * v, axis=1, keepdims=True) + NORM_EPSILON)
        one[a, b, pl.ds(r, 32), :] = (v * inv * sml[0:1, :]).astype(BF16)
        invs[a, b, pl.ds(r, 32), :] = jnp.broadcast_to(inv, (32, TILE))

    loop(16, norm_in)
    arrived(c1)
    c1 = w1b(3)
    loads["cot"].wait()
    my_row = lax.broadcasted_iota(jnp.int32, (32, D), 0) + t * BLOCK

    def mask_rows(i):
        v = cot[ty, tc, pl.ds(i * 32, 32), :].astype(F32)
        cot[ty, tc, pl.ds(i * 32, 32), :] = jnp.where(my_row + i * 32 < run, v, 0.0).astype(BF16)

    loop(4, mask_rows)
    cot_c = rows_start(cot)
    arrived(a2)

    def proj(j):
        pj[j] = mm(one[...].reshape(ROWS, D), w[:, :, :, :, at_lane(j, CH)].reshape(D, CH))

    loop(3, proj)

    def taps(k, lanes):
        return sml[2 + k : 3 + k, lanes]

    for q in range(2):
        lanes = slice(q * TILE, (q + 1) * TILE)
        own = at_lane(t * 2 + q, TILE)
        mixed = pj[0, :, lanes] * pj[2, :, lanes]
        before_one = pltpu.roll(mixed, 1, 0) * masks[0]
        before_two = pltpu.roll(mixed, 2, 0) * masks[1]
        v = taps(0, own) * mixed + taps(1, own) * before_one + taps(2, own) * before_two
        conv[:, lanes] = v
        gated[:, :, :, lanes] = (pj[1, :, lanes] * v).astype(BF16).reshape(2, 2, BLOCK, TILE)

    m_second = sum_start(0, gated, OUT_AT, CH)
    arrived(b2)
    b2 = w2b(1)
    arrived(e1)
    e2 = w2a(2)
    sum_wait(0, m_second)

    def norm_mid(i):
        r = i * 32
        v = tok[ty, tc, pl.ds(r, 32), :].astype(F32) + sum_rows(0, r, 32)
        mid[pl.ds(r, 32), :] = v
        inv = lax.rsqrt(jnp.mean(v * v, axis=1, keepdims=True) + NORM_EPSILON)
        two[ty, tc, pl.ds(r, 32), :] = (v * inv * sml[1:2, :]).astype(BF16)
        two_c.push(i)

    two_c = Pieces(two)
    loop(4, norm_mid)
    rows_relay(cot, cot_c)
    arrived(e2)
    e2 = w2b(2)
    arrived(c1)
    c2 = w2a(3)
    two_c.relay()
    two_c.wait()
    arrived(b2)

    def gate_up(i):
        lanes = pl.ds(pl.multiple_of(GU_AT + i * CH, CH), CH)
        v = mm(two[...].reshape(ROWS, D), w[:, :, :, :, lanes].reshape(D, CH))
        gate, up = v[:, :TILE], v[:, TILE:]
        s = jax.nn.sigmoid(gate)
        act = gate * s
        hid[:, :, :, at_lane(i, TILE)] = (act * up).astype(BF16).reshape(2, 2, BLOCK, TILE)
        gu[i, :, :TILE] = up * s * (1.0 + gate * (1.0 - s))
        gu[i, :, TILE:] = act

    loop(FIRST, gate_up)
    arrived(e2)
    loop(TILES - FIRST, lambda i: gate_up(i + FIRST))
    arrived(c2)
    c2 = w2b(3)
    rows_wait(cot_c)

    def wide(v):
        return v.reshape(NY, NX, SHARD, v.shape[1])

    def down_grad(i):
        a = cot[:, :, :, at_lane(i, CH)].reshape(ROWS, CH).T
        g[i, :, :, :, DOWN_AT:WIDE] = wide(mm(a, hid[...].reshape(ROWS, HID)).astype(BF16))

    loop(NZ, down_grad)
    gc_ = g2a(3)
    arrived(c2)

    def back_tile(k, gh):
        v = gu[k]
        gg[:, :, :, at_lane(2 * k, TILE)] = (gh * v[:, :TILE]).astype(BF16).reshape(2, 2, BLOCK, TILE)
        gg[:, :, :, at_lane(2 * k + 1, TILE)] = (
            (gh * v[:, TILE:]).astype(BF16).reshape(2, 2, BLOCK, TILE)
        )

    def grad_hidden(i):
        lanes = pl.ds(pl.multiple_of(DOWN_AT + i * CH, TILE), CH)
        v = mm(cot[...].reshape(ROWS, D), w[:, :, :, :, lanes].reshape(D, CH))
        back_tile(2 * i, v[:, :TILE])
        back_tile(2 * i + 1, v[:, TILE:])

    def gate_up_grad(p):
        first, n = GU_PARTS[p - 1]

        def step(i):
            a = two[:, :, :, at_lane(i, CH)].reshape(ROWS, CH).T
            b = gg[:, :, :, first * CH : (first + n) * CH].reshape(ROWS, n * CH)
            lo = GU_AT + first * CH
            g[i, :, :, :, lo : lo + n * CH] = wide(mm(a, b).astype(BF16))

        loop(NZ, step)

    loop(TILES // 2, grad_hidden)
    back_tile(
        TILES - 1,
        mm(cot[...].reshape(ROWS, D), w[:, :, :, :, WIDE - TILE : WIDE].reshape(D, TILE)),
    )
    gc_ = g2b(3, gc_)
    n_second = sum_start(1, gg, GU_AT, 2 * HID)
    gate_up_grad(1)
    gb_ = g2a(1)
    sum_wait(1, n_second)
    gacc[...] = jnp.zeros_like(gacc)

    def norm_two_back(i):
        r = i * 32
        gn = sum_rows(1, r, 32)
        v = mid[pl.ds(r, 32), :]
        inv = lax.rsqrt(jnp.mean(v * v, axis=1, keepdims=True) + NORM_EPSILON)
        unit = v * inv
        gacc[1:2, :] += jnp.sum(gn * unit, axis=0, keepdims=True)
        scaled = gn * sml[1:2, :]
        inner = jnp.mean(scaled * unit, axis=1, keepdims=True)
        out = cot[ty, tc, pl.ds(r, 32), :].astype(F32) + inv * (scaled - unit * inner)
        gmid[pl.ds(r, 32), :] = out
        rmid[ty, tc, pl.ds(r, 32), :] = out.astype(BF16)
        mid_c.push(i)

    mid_c = Pieces(rmid)
    loop(4, norm_two_back)
    gate_up_grad(2)
    ge_ = g2a(2)
    gc_ = g1a(3, gc_)
    mid_c.relay()
    gb_ = g2b(1, gb_)
    mid_c.wait()

    pg = mm(rmid[...].reshape(ROWS, D), w[:, :, :, :, OUT_AT : OUT_AT + CH].reshape(D, CH))
    for q in range(2):
        lanes = slice(q * TILE, (q + 1) * TILE)
        own = at_lane(t * 2 + q, TILE)
        gate_b, gate_c, values = pj[0, :, lanes], pj[1, :, lanes], pj[2, :, lanes]
        mixed = gate_b * values
        gv = pg[:, lanes]
        grad_c = gv * conv[:, lanes]
        grad_conv = gv * gate_c
        one_grad, two_grad = grad_conv * masks[0], grad_conv * masks[1]
        gacc[2:3, own] = jnp.sum(grad_conv * mixed, axis=0, keepdims=True)
        gacc[3:4, own] = jnp.sum(one_grad * pltpu.roll(mixed, 1, 0), axis=0, keepdims=True)
        gacc[4:5, own] = jnp.sum(two_grad * pltpu.roll(mixed, 2, 0), axis=0, keepdims=True)
        grad_mixed = (
            taps(0, own) * grad_conv
            + taps(1, own) * pltpu.roll(one_grad, ROWS - 1, 0)
            + taps(2, own) * pltpu.roll(two_grad, ROWS - 2, 0)
        )
        for j, v in enumerate((grad_mixed * values, grad_c, grad_mixed * gate_b)):
            lo = j * CH + q * TILE
            gp[:, :, :, lo : lo + TILE] = v.astype(BF16).reshape(2, 2, BLOCK, TILE)

    i_second = sum_start(3, gp, 0, 3 * CH)

    def mix_grad(i):
        a = one[:, :, :, at_lane(i, CH)].reshape(ROWS, CH).T
        g[i, :, :, :, :OUT_AT] = wide(mm(a, gp[...].reshape(ROWS, 3 * CH)).astype(BF16))
        b = rmid[:, :, :, at_lane(i, CH)].reshape(ROWS, CH).T
        g[i, :, :, :, OUT_AT:GU_AT] = wide(mm(b, gated[...].reshape(ROWS, CH)).astype(BF16))

    loop(NZ, mix_grad)
    ga_ = g2a(0)

    def gain_one(i):
        lanes = at_lane(i, CH)
        out = jnp.zeros((1, CH), F32)
        for c, terms in ((1 - tc, ps), (tc, po)):
            for a in range(2):
                unit = tok[a, c, :, lanes].astype(F32) * jnp.tile(invs[a, c], (1, 2))
                out += jnp.sum(terms[3, i, a].astype(F32) * unit, axis=0, keepdims=True)
        gacc[0:1, lanes] = out

    loop(NZ, gain_one)
    for k in range(8):
        sgr[k // 2, k % 2] = gacc[:, k * TILE : (k + 1) * TILE]
    u_z = [
        links.push(sgr.at[zz], gr.at[i], to)
        for i, (zz, to) in enumerate(((zp, to_zp), (zo, to_zo), (zm, to_zm)))
    ]
    ge_ = g2b(2, ge_)
    gb_ = g1a(1, gb_)
    gc_ = g1b(3, gc_)
    arrived(u_z)
    sgr[z] = sgr[z] + gr[0] + gr[1] + gr[2]
    u_y = links.push(sgr.at[z, 1 - yh], gc.at[0], to_y)
    sum_wait(3, i_second)

    def norm_one_back(i):
        r = i * 32
        gn = sum_rows(3, r, 32)
        unit = tok[ty, tc, pl.ds(r, 32), :].astype(F32)
        inv = lax.rsqrt(jnp.mean(unit * unit, axis=1, keepdims=True) + NORM_EPSILON)
        unit = unit * inv
        scaled = gn * sml[0:1, :]
        inner = jnp.mean(scaled * unit, axis=1, keepdims=True)
        tg[pl.ds(r, 32), :] = gmid[pl.ds(r, 32), :] + inv * (scaled - unit * inner)

    loop(4, norm_one_back)
    store(tg, tg_out)
    ga_ = g2b(0, ga_)
    gb_ = g1b(1, gb_)
    u_y.wait_recv()
    gc[1] = sgr[z, yh] + gc[0]
    u_x = tile_send(gc.at[1], gc, 2, x_peers)
    o_second = sum_start(2, hid, DOWN_AT, HID)
    ge_ = g1a(2, ge_)
    gc_ = gy(3, gc_)
    gc[5] = tile_sum(gc[1], gc, 2, u_x)
    u_t = tile_send(gc.at[5], gc, 6, tensor_peers)
    ga_ = g1_all(0, ga_)
    gb_ = gy(1, gb_)
    ge_ = g1b(2, ge_)
    sum_wait(2, o_second)

    def out_rows(i):
        r = i * 32
        bo[pl.ds(r, 32), :] = (mid[pl.ds(r, 32), :] + sum_rows(2, r, 32)).astype(BF16)

    loop(4, out_rows)
    store(bo, bo_out)
    gend(3, gc_)
    ga_ = gy_all(0, ga_)
    ge_ = gy(2, ge_)
    gend(1, gb_)
    gc[9] = pltpu.roll(tile_sum(gc[5], gc, 6, u_t), TILE - place, 1)
    for j in (1, 2):
        loads[0, j].wait()
    update(0, (), gc[9, 0:5, 0:8], RATE_SMALL)
    put(0)
    gend(2, ge_)
    gend(0, ga_)
    for c in links.open:
        c.wait_send()
    for c in stores:
        c.wait()


N_COPIES = 240


def train_call(lengths, tokens, cotangent, *state):
    anywhere = pl.BlockSpec(memory_space=pltpu.HBM)
    rows = (2, 2, BLOCK)
    weights = state[:5]
    out_shape = [jax.ShapeDtypeStruct((BLOCK, D), BF16), jax.ShapeDtypeStruct((BLOCK, D), F32)]
    for v in weights:
        out_shape += [jax.ShapeDtypeStruct(v.shape, F32)] * 3
    return pl.pallas_call(
        train_kernel,
        out_shape=out_shape,
        in_specs=[pl.BlockSpec(memory_space=pltpu.SMEM)] + [anywhere] * 17,
        out_specs=[anywhere] * 17,
        scratch_shapes=[pltpu.VMEM((3,) + v.shape, F32) for v in weights]
        + [
            pltpu.VMEM((BLOCK, D), BF16),
            pltpu.VMEM((BLOCK, D), F32),
            pltpu.SemaphoreType.DMA((40,)),
            pltpu.VMEM((NZ, NY, NX, SHARD, WIDE), BF16),
            pltpu.VMEM((NZ, NY, NX, SHARD, WIDE), BF16),
            pltpu.VMEM(rows + (D,), BF16),
            pltpu.VMEM(rows + (D,), BF16),
            pltpu.VMEM(rows + (D,), BF16),
            pltpu.VMEM(rows + (D,), BF16),
            pltpu.VMEM(rows + (D,), BF16),
            pltpu.VMEM((2, ROWS, TILE), F32),
            pltpu.VMEM((3, ROWS, CH), F32),
            pltpu.VMEM((ROWS, CH), F32),
            pltpu.VMEM(rows + (CH,), BF16),
            pltpu.VMEM(rows + (3 * CH,), BF16),
            pltpu.VMEM((TILES, ROWS, CH), F32),
            pltpu.VMEM(rows + (HID,), BF16),
            pltpu.VMEM(rows + (2 * HID,), BF16),
            pltpu.VMEM((BLOCK, D), F32),
            pltpu.VMEM((BLOCK, D), F32),
            pltpu.VMEM((8, D), F32),
            pltpu.VMEM((2, 8, TILE), F32),
            pltpu.VMEM((6, 8, TILE), F32),
            pltpu.VMEM((NZ, NY, 8, TILE), F32),
            pltpu.VMEM((NZ, NY, 8, TILE), F32),
            pltpu.VMEM((3, NY, 8, TILE), F32),
            pltpu.VMEM((10, 8, TILE), F32),
            pltpu.VMEM((8, D), F32),
            pltpu.VMEM(rows + (TILE,), F32),
            pltpu.VMEM((4, NZ, 2, BLOCK, CH), BF16),
            pltpu.VMEM((4, NZ, 2, BLOCK, CH), BF16),
            pltpu.VMEM((4, NZ, 2, BLOCK, CH), F32),
            pltpu.VMEM((4, NZ, BLOCK, CH), BF16),
            pltpu.VMEM((4, NZ, BLOCK, CH), BF16),
            pltpu.VMEM((2, 2, 4, HALF, WIDE), BF16),
            pltpu.VMEM((2, NY, NX, HALF, WIDE), BF16),
            pltpu.VMEM((2, NZ, NY, HALF, WIDE), BF16),
            pltpu.VMEM((2, 2, HALF, WIDE), BF16),
            pltpu.VMEM((2, 3, 2, HALF, WIDE), BF16),
            pltpu.VMEM((SHARD, WIDE), BF16),
            pltpu.SemaphoreType.DMA((N_COPIES,)),
            pltpu.SemaphoreType.DMA((N_COPIES,)),
        ],
        compiler_params=pltpu.CompilerParams(
            collective_id=0, has_side_effects=True, vmem_limit_bytes=63 * 1024 * 1024
        ),
        cost_estimate=pl.CostEstimate(
            flops=6 * ROWS * D * WIDE, bytes_accessed=8 * 1024 * 1024, transcendentals=ROWS * HID
        ),
    )(lengths, tokens, cotangent, *state)


def hand_over(*refs):
    n = (len(refs) - 2) // 3
    sources, targets, held = refs[:n], refs[n : 2 * n], refs[2 * n : 3 * n]
    load_sem, store_sem = refs[3 * n :]
    loads = [pltpu.make_async_copy(sources[i], held[i], load_sem.at[i]) for i in range(n)]
    stores = [pltpu.make_async_copy(held[i], targets[i], store_sem.at[i]) for i in range(n)]
    for c in loads:
        c.start()
    for i in range(n):
        loads[i].wait()
        stores[i].start()
    for c in stores:
        c.wait()


def per_device(
    tokens,
    cotangent,
    lengths,
    small,
    mix_in,
    mix_out,
    ffn_gate_up,
    ffn_down,
    small_first,
    small_second,
    in_first,
    in_second,
    out_first,
    out_second,
    gate_up_first,
    gate_up_second,
    down_first,
    down_second,
):
    found = train_call(
        lengths,
        tokens,
        cotangent,
        small,
        mix_in,
        mix_out,
        ffn_gate_up,
        ffn_down,
        small_first,
        small_second,
        in_first,
        in_second,
        out_first,
        out_second,
        gate_up_first,
        gate_up_second,
        down_first,
        down_second,
    )
    anywhere = pl.BlockSpec(memory_space=pltpu.HBM)
    n = len(found)
    return tuple(
        pl.pallas_call(
            hand_over,
            out_shape=[jax.ShapeDtypeStruct(v.shape, v.dtype) for v in found],
            in_specs=[anywhere] * n,
            out_specs=[anywhere] * n,
            scratch_shapes=[pltpu.VMEM(v.shape, v.dtype) for v in found]
            + [pltpu.SemaphoreType.DMA((n,))] * 2,
        )(*found)
    )


def solution(mesh):
    rows = P(("dp", "tensor"), None)
    small = P(None, ("dp", "tensor"))
    deep = P(None, "dp", "tensor")
    flat = P("dp", "tensor")
    in_specs = (rows, rows, P("dp", None), small, deep, flat, deep, flat)
    in_specs += (small,) * 2 + (deep,) * 2 + (flat,) * 2 + (deep,) * 2 + (flat,) * 2
    out_specs = (rows, rows) + (small,) * 3 + (deep,) * 3 + (flat,) * 3 + (deep,) * 3 + (flat,) * 3
    return jax.shard_map(
        per_device, mesh=mesh, in_specs=in_specs, out_specs=out_specs, check_vma=False
    )
```

```python
import functools

import jax
import jax.numpy as jnp
from jax import lax
from jax.experimental import pallas as pl
from jax.experimental.pallas import tpu as pltpu
from jax.sharding import PartitionSpec as P

STEP = 10
NORM_EPSILON = 1e-05
BETA_FIRST = 0.9
BETA_SECOND = 0.95
ADAM_EPSILON = 1e-08
DECAY_RATE = 0.1
RATE_PROJ = 0.1
RATE_DOWN = 0.045
RATE_SMALL = 0.6

MESH = pl.DeviceIdType.MESH
F32 = jnp.float32
BF16 = jnp.bfloat16

D = 1024
ROWS = 512
BLOCK = 128
CH = 256
HID = 1152
TILE = 128
TILES = HID // TILE
OUT_AT = 3 * CH
GU_AT = 4 * CH
DOWN_AT = GU_AT + 2 * HID
WIDE = DOWN_AT + HID
FIRST = TILES // 2
GU_PARTS = ((0, FIRST), (FIRST, TILES - FIRST))
PARTS = (
    (0, GU_AT),
    (GU_AT, FIRST * CH),
    (GU_AT + FIRST * CH, (TILES - FIRST) * CH),
    (DOWN_AT, HID),
)
NZ, NY, NX, SHARD = 4, 2, 4, 32
HALF = SHARD // 2


def mm(a, b):
    return lax.dot_general(a, b, (((1,), (0,)), ((), ())), preferred_element_type=F32)


def mm_nt(a, b):
    return lax.dot_general(a, b, (((1,), (1,)), ((), ())), preferred_element_type=F32)


def loop(n, body):
    lax.fori_loop(0, n, lambda i, carry: (body(i), carry)[1], 0)


def at_lane(i, width):
    return pl.ds(pl.multiple_of(i * width, width), width)


def adam_step(weight, grad, first, second, rate):
    first_new = BETA_FIRST * first + (1.0 - BETA_FIRST) * grad
    second_new = BETA_SECOND * second + (1.0 - BETA_SECOND) * grad * grad
    first_hat = first_new / (1.0 - BETA_FIRST**STEP)
    second_hat = second_new / (1.0 - BETA_SECOND**STEP)
    weight_new = weight - rate * (
        first_hat / (jnp.sqrt(second_hat) + ADAM_EPSILON) + DECAY_RATE * weight
    )
    return (first_new, second_new, weight_new)


class Links:
    def __init__(self, send, recv):
        self.send, self.recv, self.used, self.open = send, recv, 0, []

    def take(self, n=1):
        first = self.used
        self.used += n
        return first

    def copy(self, src, dst, to, slot):
        return pltpu.make_async_remote_copy(
            src_ref=src,
            dst_ref=dst,
            send_sem=self.send.at[slot],
            recv_sem=self.recv.at[slot],
            device_id=to,
            device_id_type=MESH,
        )

    def push(self, src, dst, to):
        c = self.copy(src, dst, to, self.take())
        c.start()
        self.open.append(c)
        return c


def arrived(copies):
    for c in copies:
        c.wait_recv()


def train_kernel(*refs):
    lens, tok_in, cot_in = refs[:3]
    state_in = refs[3:18]
    bo_out, tg_out = refs[18:20]
    state_out = refs[20:35]
    train_body(lens, tok_in, cot_in, state_in, bo_out, tg_out, state_out, *refs[35:])


def train_body(
    lens,
    tok_in,
    cot_in,
    state_in,
    bo_out,
    tg_out,
    state_out,
    state_small,
    state_in_w,
    state_out_w,
    state_gu,
    state_down,
    bo,
    tg,
    local_sem,
    w,
    g,
    tok,
    cot,
    one,
    two,
    rmid,
    masks,
    pj,
    conv,
    gated,
    gp,
    gu,
    hid,
    gg,
    mid,
    gmid,
    sml,
    st,
    sr,
    sm,
    sgr,
    gr,
    gc,
    gacc,
    invs,
    ps,
    pr,
    po,
    qs,
    qr,
    r2s1,
    r2s2z,
    r2s2x,
    r1s1,
    r1s2,
    ry,
    send_sem,
    recv_sem,
):
    dp = lax.axis_index("dp")
    t = lax.axis_index("tensor")
    z, yh, x = dp // 8, (dp // 4) % 2, dp % 4
    ty, tc = t // 2, t % 2
    zp, zm, zo = (z + 1) % 4, (z + 3) % 4, (z + 2) % 4
    xp, xm, xo = (x + 1) % 4, (x + 3) % 4, (x + 2) % 4

    def at(zz, yy, xx):
        return (zz * 8 + yy * 4 + xx, t)

    to_y = at(z, 1 - yh, x)
    to_xp, to_xm = at(z, yh, xp), at(z, yh, xm)
    to_zp, to_zm = at(zp, yh, x), at(zm, yh, x)
    to_xo, to_zo = at(z, yh, xo), at(zo, yh, x)
    to_core = (dp, ty * 2 + 1 - tc)
    to_far = (dp, (1 - ty) * 2 + tc)
    to_across = (dp, (1 - ty) * 2 + 1 - tc)
    tensor_peers = (to_core, to_far, to_across)
    x_peers = (to_xp, to_xo, to_xm)
    z_peers = (to_zp, to_zo, to_zm)
    links = Links(send_sem, recv_sem)

    barrier = pltpu.get_barrier_semaphore()
    peers = (to_y, to_xp, to_xm, to_xo, to_zp, to_zm, to_zo, to_core, to_far, to_across)
    for to in peers:
        pl.semaphore_signal(barrier, inc=1, device_id=to, device_id_type=MESH)

    state = (state_small, state_in_w, state_out_w, state_gu, state_down)
    n_local = 0
    loads = {}
    for key, src, dst in (
        [((k, 0), state_in[k], state[k].at[0]) for k in range(5)]
        + [("tok", tok_in, tok.at[ty, tc]), ("cot", cot_in, cot.at[ty, tc])]
        + [((k, j), state_in[3 + 2 * k + j + 1], state[k].at[j]) for k in range(5) for j in (1, 2)]
    ):
        loads[key] = pltpu.make_async_copy(src, dst, local_sem.at[n_local])
        loads[key].start()
        n_local += 1
    stores = []

    def store(src, dst):
        c = pltpu.make_async_copy(src, dst, local_sem.at[n_local + len(stores)])
        c.start()
        stores.append(c)

    row = lax.broadcasted_iota(jnp.int32, (ROWS, TILE), 0)
    start = jnp.zeros((ROWS, TILE), jnp.int32)
    run = jnp.int32(0)
    for k in range(lens.shape[1]):
        run = run + lens[0, k]
        start = jnp.where(row >= run, run, start)
    dist = row - start
    masks[0] = jnp.where(dist >= 1, 1.0, 0.0)
    masks[1] = jnp.where(dist >= 2, 1.0, 0.0)

    place = ((dp % 4) * 4 + t) * 8
    st[0] = jnp.zeros((8, TILE), F32)
    loads[0, 0].wait()
    st[0, 0:5, 0:8] = state_small[0]
    st[0] = pltpu.roll(st[0], place, 1)
    loads[1, 0].wait()
    for j in range(3):
        w[z, yh, x, :, j * CH : (j + 1) * CH] = state_in_w[0, j].astype(BF16)
    loads[2, 0].wait()
    w[z, yh, x, :, OUT_AT : OUT_AT + CH] = state_out_w[0].astype(BF16)
    loads[3, 0].wait()
    for i in range(TILES):
        for j in range(2):
            lo = GU_AT + (2 * i + j) * TILE
            w[z, yh, x, :, lo : lo + TILE] = state_gu[0, j, :, i * TILE : (i + 1) * TILE].astype(BF16)
    loads[4, 0].wait()
    w[z, yh, x, :, DOWN_AT:WIDE] = state_down[0].astype(BF16)
    loads["tok"].wait()
    pl.semaphore_wait(barrier, len(peers))

    lo_half, hi_half = pl.ds(0, HALF), pl.ds(HALF, HALF)

    def cols(part):
        return pl.ds(PARTS[part][0], PARTS[part][1])

    def same(ref, to):
        return links.push(ref, ref, to)

    def wy(p):
        return same(w.at[z, yh, x, :, cols(p)], to_y)

    def w1a(p):
        a, b = w.at[z, :, x, lo_half, cols(p)], w.at[z, :, x, hi_half, cols(p)]
        return [same(a, to_xp), same(a, to_xm), same(b, to_zp), same(b, to_zm)]

    def w1_all(p):
        a, b = w.at[z, :, x, lo_half, cols(p)], w.at[z, :, x, hi_half, cols(p)]
        return [same(a, to) for to in x_peers] + [same(b, to) for to in z_peers]

    def w1b(p):
        return [
            same(w.at[z, 0, xm, lo_half, cols(p)], to_xp),
            same(w.at[z, 1, xp, lo_half, cols(p)], to_xm),
            same(w.at[zm, 0, x, hi_half, cols(p)], to_zp),
            same(w.at[zp, 1, x, hi_half, cols(p)], to_zm),
        ]

    def w2a(p):
        a, b = w.at[z, :, :, lo_half, cols(p)], w.at[:, :, x, hi_half, cols(p)]
        return [same(a, to_zp), same(a, to_zm), same(b, to_xp), same(b, to_xm)]

    def w2b(p):
        return [
            same(w.at[zm, 0, :, lo_half, cols(p)], to_zp),
            same(w.at[zp, 1, :, lo_half, cols(p)], to_zm),
            same(w.at[:, 0, xm, hi_half, cols(p)], to_xp),
            same(w.at[:, 1, xp, hi_half, cols(p)], to_xm),
        ]

    def rows_start(ref):
        mine = ref.at[ty, tc]
        return [same(mine, to_far), same(mine, to_core)]

    def rows_relay(ref, copies):
        copies[0].wait_recv()
        copies.append(same(ref.at[1 - ty, tc], to_core))

    def rows_wait(copies):
        arrived(copies[1:])

    def piece(i):
        return pl.ds(i * (BLOCK // NZ), BLOCK // NZ)

    class Pieces:
        def __init__(self, ref):
            self.ref, self.first = ref, links.take(3 * NZ)

        def part(self, kind, i):
            mine = self.ref.at[(1 - ty) if kind == 2 else ty, tc, piece(i)]
            to = to_far if kind == 0 else to_core
            return links.copy(mine, mine, to, self.first + kind * NZ + i)

        def push(self, i):
            self.part(0, i).start()
            self.part(1, i).start()

        def relay(self):
            def step(i):
                self.part(0, i).wait_recv()
                self.part(2, i).start()

            loop(NZ, step)

        def wait(self):
            for i in range(NZ):
                self.part(1, i).wait_recv()
                self.part(2, i).wait_recv()
            links.open += [self.part(kind, i) for kind in range(3) for i in range(NZ)]

    def sum_start(u, lhs, lo, k):
        first, second = links.take(NZ), links.take(NZ)

        def near(i):
            return links.copy(ps.at[u, i], pr.at[u, i], to_core, first + i)

        def far(i):
            return links.copy(qs.at[u, i], qr.at[u, i], to_far, second + i)

        def step(i):
            wt = w[i, :, :, :, lo : lo + k].reshape(D // NZ, k)
            a = lhs[:, 1 - tc].reshape(2 * BLOCK, k)
            ps[u, i] = mm_nt(a, wt).astype(BF16).reshape(2, BLOCK, CH)
            near(i).start()
            b = lhs[:, tc].reshape(2 * BLOCK, k)
            po[u, i] = mm_nt(b, wt).reshape(2, BLOCK, CH)

        def cross(i):
            near(i).wait_recv()
            other = po[u, i, 1 - ty] + pr[u, i, 1 - ty].astype(F32)
            qs[u, i] = other.astype(BF16)
            far(i).start()

        def both(i):
            step(i + 1)
            cross(i)

        step(0)
        loop(NZ - 1, both)
        cross(NZ - 1)
        links.open += [near(i) for i in range(NZ)] + [far(i) for i in range(NZ)]
        return second

    def sum_wait(u, second):
        for i in range(NZ):
            links.copy(qs.at[u, i], qr.at[u, i], to_far, second + i).wait_recv()

    def sum_rows(u, lo, n):
        return jnp.concatenate(
            [
                po[u, i, ty, pl.ds(lo, n), :]
                + pr[u, i, ty, pl.ds(lo, n), :].astype(F32)
                + qr[u, i, pl.ds(lo, n), :].astype(F32)
                for i in range(NZ)
            ],
            axis=1,
        )

    def add_to(dst, src):
        dst[...] = (dst[...].astype(F32) + src[...].astype(F32)).astype(BF16)

    def g2a(p):
        c = cols(p)
        return [
            links.push(g.at[zo, 0, :, lo_half, c], r2s1.at[0, 0, :, :, c], to_zm),
            links.push(g.at[zo, 1, :, lo_half, c], r2s1.at[0, 1, :, :, c], to_zp),
            links.push(g.at[:, 0, xo, hi_half, c], r2s1.at[1, 0, :, :, c], to_xm),
            links.push(g.at[:, 1, xo, hi_half, c], r2s1.at[1, 1, :, :, c], to_xp),
        ]

    def g2b(p, copies):
        c = cols(p)
        out = []
        for k, (y, zz, to) in enumerate(((0, zm, to_zm), (1, zp, to_zp))):
            copies[k].wait_recv()
            loop(4, lambda i: add_to(g.at[zz, y, i, lo_half, c], r2s1.at[0, y, i, :, c]))
            out.append(links.push(g.at[zz, :, :, lo_half, c], r2s2z.at[y, :, :, :, c], to))
        for k, (y, xx, to) in enumerate(((0, xm, to_xm), (1, xp, to_xp))):
            copies[2 + k].wait_recv()
            loop(4, lambda i: add_to(g.at[i, y, xx, hi_half, c], r2s1.at[1, y, i, :, c]))
            out.append(links.push(g.at[:, :, xx, hi_half, c], r2s2x.at[y, :, :, :, c], to))
        return out

    def add_two(dst, a, b):
        total = dst[...].astype(F32) + a[...].astype(F32) + b[...].astype(F32)
        dst[...] = total.astype(BF16)

    def g1a(p, copies):
        c = cols(p)
        arrived(copies[:2])
        loop(
            8,
            lambda i: add_two(
                g.at[z, i // 4, i % 4, lo_half, c],
                r2s2z.at[0, i // 4, i % 4, :, c],
                r2s2z.at[1, i // 4, i % 4, :, c],
            ),
        )
        out = [
            links.push(g.at[z, 0, xo, lo_half, c], r1s1.at[0, 0, :, c], to_xm),
            links.push(g.at[z, 1, xo, lo_half, c], r1s1.at[0, 1, :, c], to_xp),
        ]
        arrived(copies[2:])
        loop(
            8,
            lambda i: add_two(
                g.at[i // 2, i % 2, x, hi_half, c],
                r2s2x.at[0, i // 2, i % 2, :, c],
                r2s2x.at[1, i // 2, i % 2, :, c],
            ),
        )
        return out + [
            links.push(g.at[zo, 0, x, hi_half, c], r1s1.at[1, 0, :, c], to_zm),
            links.push(g.at[zo, 1, x, hi_half, c], r1s1.at[1, 1, :, c], to_zp),
        ]

    def sum_second(p, copies):
        c = cols(p)
        arrived(copies)
        loop(
            8,
            lambda i: add_two(
                g.at[z, i // 4, i % 4, lo_half, c],
                r2s2z.at[0, i // 4, i % 4, :, c],
                r2s2z.at[1, i // 4, i % 4, :, c],
            ),
        )
        loop(
            8,
            lambda i: add_two(
                g.at[i // 2, i % 2, x, hi_half, c],
                r2s2x.at[0, i // 2, i % 2, :, c],
                r2s2x.at[1, i // 2, i % 2, :, c],
            ),
        )

    def g1_all(p, copies):
        c = cols(p)
        sum_second(p, copies)
        out = []
        for i, (xx, to) in enumerate(((xp, to_xp), (xo, to_xo), (xm, to_xm))):
            out.append(links.push(g.at[z, :, xx, lo_half, c], r1s2.at[0, i, :, :, c], to))
        for i, (zz, to) in enumerate(((zp, to_zp), (zo, to_zo), (zm, to_zm))):
            out.append(links.push(g.at[zz, :, x, hi_half, c], r1s2.at[1, i, :, :, c], to))
        return out

    def gy_all(p, copies):
        c = cols(p)
        arrived(copies)
        for h, rows in enumerate((lo_half, hi_half)):
            for y in range(2):
                total = g[z, y, x, rows, c].astype(F32)
                for i in range(3):
                    total = total + r1s2[h, i, y, :, c].astype(F32)
                g[z, y, x, rows, c] = total.astype(BF16)
        return links.push(g.at[z, 1 - yh, x, :, c], ry.at[:, c], to_y)

    def g1b(p, copies):
        c = cols(p)
        out = []
        for k, (y, xx, to) in enumerate(((0, xm, to_xm), (1, xp, to_xp))):
            copies[k].wait_recv()
            add_to(g.at[z, y, xx, lo_half, c], r1s1.at[0, y, :, c])
            out.append(links.push(g.at[z, :, xx, lo_half, c], r1s2.at[0, y, :, :, c], to))
        for k, (y, zz, to) in enumerate(((0, zm, to_zm), (1, zp, to_zp))):
            copies[2 + k].wait_recv()
            add_to(g.at[zz, y, x, hi_half, c], r1s1.at[1, y, :, c])
            out.append(links.push(g.at[zz, :, x, hi_half, c], r1s2.at[1, y, :, :, c], to))
        return out

    def gy(p, copies):
        c = cols(p)
        arrived(copies)
        for h, rows in enumerate((lo_half, hi_half)):
            loop(
                2,
                lambda y: add_two(
                    g.at[z, y, x, rows, c], r1s2.at[h, 0, y, :, c], r1s2.at[h, 1, y, :, c]
                ),
            )
        return links.push(g.at[z, 1 - yh, x, :, c], ry.at[:, c], to_y)

    def update(k, where, grad, rate):
        ref = state[k]
        found = adam_step(ref[(0, *where)], grad, ref[(1, *where)], ref[(2, *where)], rate)
        for j, value in enumerate(found):
            ref[((1, 2, 0)[j], *where)] = value

    def put(k):
        for j in range(3):
            store(state[k].at[(1, 2, 0)[j]], state_out[3 * k + j])

    def total(lo, n):
        return g[z, yh, x, :, lo : lo + n].astype(F32) + ry[:, lo : lo + n].astype(F32)

    def gend(p, copy):
        copy.wait_recv()
        if p == 0:
            for k in (1, 2):
                for j in (1, 2):
                    loads[k, j].wait()
            for j in range(3):
                update(1, (j,), total(j * CH, CH), RATE_PROJ)
            update(2, (), total(OUT_AT, CH), RATE_PROJ)
            put(1)
            put(2)
        elif p < 3:
            if p == 1:
                for j in (1, 2):
                    loads[3, j].wait()
            first, n = GU_PARTS[p - 1]
            for i in range(first, first + n):
                for j in range(2):
                    where = (j, slice(None), slice(i * TILE, (i + 1) * TILE))
                    update(3, where, total(GU_AT + (2 * i + j) * TILE, TILE), RATE_PROJ)
            if p == 2:
                put(3)
        else:
            for j in (1, 2):
                loads[4, j].wait()
            update(4, (), total(DOWN_AT, HID), RATE_DOWN)
            put(4)


    def tile_send(src, slots, first, to_all):
        return [links.push(src, slots.at[first + i], to) for i, to in enumerate(to_all)]

    def tile_sum(own, slots, first, copies):
        arrived(copies)
        return own + slots[first] + slots[first + 1] + slots[first + 2]

    s_t = tile_send(st.at[0], sr, 0, tensor_peers)
    ya = wy(0)
    yb = wy(1)
    ye = wy(2)
    yc = wy(3)
    tok_c = rows_start(tok)
    st[1] = tile_sum(st[0], sr, 0, s_t)
    s_x = tile_send(st.at[1], sr, 3, x_peers)
    ya.wait_recv()
    a1 = w1_all(0)
    sm[z, yh] = tile_sum(st[1], sr, 3, s_x)
    s_y = same(sm.at[z, yh], to_y)
    yb.wait_recv()
    b1 = w1a(1)
    arrived(a1)
    a2 = w2a(0)
    s_y.wait_recv()
    s_z = [same(sm.at[z], to) for to in z_peers]
    ye.wait_recv()
    e1 = w1a(2)
    arrived(b1)
    b1 = w1b(1)
    yc.wait_recv()
    c1 = w1a(3)
    arrived(e1)
    e1 = w1b(2)
    rows_relay(tok, tok_c)
    arrived(s_z)
    for k in range(8):
        sml[:, k * TILE : (k + 1) * TILE] = sm[k // 2, k % 2]
    arrived(b1)
    arrived(a2)
    a2 = w2b(0)
    b2 = w2a(1)
    rows_wait(tok_c)

    def norm_in(i):
        a, b, r = i // 8, (i // 4) % 2, (i % 4) * 32
        v = tok[a, b, pl.ds(r, 32), :].astype(F32)
        inv = lax.rsqrt(jnp.mean(v * v, axis=1, keepdims=True) + NORM_EPSILON)
        one[a, b, pl.ds(r, 32), :] = (v * inv * sml[0:1, :]).astype(BF16)
        invs[a, b, pl.ds(r, 32), :] = jnp.broadcast_to(inv, (32, TILE))

    loop(16, norm_in)
    arrived(c1)
    c1 = w1b(3)
    loads["cot"].wait()
    my_row = lax.broadcasted_iota(jnp.int32, (32, D), 0) + t * BLOCK

    def mask_rows(i):
        v = cot[ty, tc, pl.ds(i * 32, 32), :].astype(F32)
        cot[ty, tc, pl.ds(i * 32, 32), :] = jnp.where(my_row + i * 32 < run, v, 0.0).astype(BF16)

    loop(4, mask_rows)
    cot_c = rows_start(cot)
    arrived(a2)

    def proj(j):
        pj[j] = mm(one[...].reshape(ROWS, D), w[:, :, :, :, at_lane(j, CH)].reshape(D, CH))

    loop(3, proj)

    def taps(k, lanes):
        return sml[2 + k : 3 + k, lanes]

    for q in range(2):
        lanes = slice(q * TILE, (q + 1) * TILE)
        own = at_lane(t * 2 + q, TILE)
        mixed = pj[0, :, lanes] * pj[2, :, lanes]
        before_one = pltpu.roll(mixed, 1, 0) * masks[0]
        before_two = pltpu.roll(mixed, 2, 0) * masks[1]
        v = taps(0, own) * mixed + taps(1, own) * before_one + taps(2, own) * before_two
        conv[:, lanes] = v
        gated[:, :, :, lanes] = (pj[1, :, lanes] * v).astype(BF16).reshape(2, 2, BLOCK, TILE)

    arrived(b2)
    b2 = w2b(1)
    arrived(e1)
    e2 = w2a(2)
    m_second = sum_start(0, gated, OUT_AT, CH)
    sum_wait(0, m_second)

    def norm_mid(i):
        r = i * 32
        v = tok[ty, tc, pl.ds(r, 32), :].astype(F32) + sum_rows(0, r, 32)
        mid[pl.ds(r, 32), :] = v
        inv = lax.rsqrt(jnp.mean(v * v, axis=1, keepdims=True) + NORM_EPSILON)
        two[ty, tc, pl.ds(r, 32), :] = (v * inv * sml[1:2, :]).astype(BF16)
        two_c.push(i)

    two_c = Pieces(two)
    loop(4, norm_mid)
    rows_relay(cot, cot_c)
    arrived(e2)
    e2 = w2b(2)
    arrived(c1)
    c2 = w2a(3)
    two_c.relay()
    two_c.wait()
    arrived(b2)

    def gate_up(i):
        lanes = pl.ds(pl.multiple_of(GU_AT + i * CH, CH), CH)
        v = mm(two[...].reshape(ROWS, D), w[:, :, :, :, lanes].reshape(D, CH))
        gate, up = v[:, :TILE], v[:, TILE:]
        s = jax.nn.sigmoid(gate)
        act = gate * s
        hid[:, :, :, at_lane(i, TILE)] = (act * up).astype(BF16).reshape(2, 2, BLOCK, TILE)
        gu[i, :, :TILE] = up * s * (1.0 + gate * (1.0 - s))
        gu[i, :, TILE:] = act

    loop(FIRST, gate_up)
    arrived(e2)
    loop(TILES - FIRST, lambda i: gate_up(i + FIRST))
    arrived(c2)
    c2 = w2b(3)
    rows_wait(cot_c)

    def wide(v):
        return v.reshape(NY, NX, SHARD, v.shape[1])

    def down_grad(i):
        a = cot[:, :, :, at_lane(i, CH)].reshape(ROWS, CH).T
        g[i, :, :, :, DOWN_AT:WIDE] = wide(mm(a, hid[...].reshape(ROWS, HID)).astype(BF16))

    loop(NZ, down_grad)
    gc_ = g2a(3)
    arrived(c2)

    def back_tile(k, gh):
        v = gu[k]
        gg[:, :, :, at_lane(2 * k, TILE)] = (gh * v[:, :TILE]).astype(BF16).reshape(2, 2, BLOCK, TILE)
        gg[:, :, :, at_lane(2 * k + 1, TILE)] = (
            (gh * v[:, TILE:]).astype(BF16).reshape(2, 2, BLOCK, TILE)
        )

    def grad_hidden(i):
        lanes = pl.ds(pl.multiple_of(DOWN_AT + i * CH, TILE), CH)
        v = mm(cot[...].reshape(ROWS, D), w[:, :, :, :, lanes].reshape(D, CH))
        back_tile(2 * i, v[:, :TILE])
        back_tile(2 * i + 1, v[:, TILE:])

    def gate_up_grad(p):
        first, n = GU_PARTS[p - 1]

        def step(i):
            a = two[:, :, :, at_lane(i, CH)].reshape(ROWS, CH).T
            b = gg[:, :, :, first * CH : (first + n) * CH].reshape(ROWS, n * CH)
            lo = GU_AT + first * CH
            g[i, :, :, :, lo : lo + n * CH] = wide(mm(a, b).astype(BF16))

        loop(NZ, step)

    loop(TILES // 2, grad_hidden)
    back_tile(
        TILES - 1,
        mm(cot[...].reshape(ROWS, D), w[:, :, :, :, WIDE - TILE : WIDE].reshape(D, TILE)),
    )
    gc_ = g2b(3, gc_)
    n_second = sum_start(1, gg, GU_AT, 2 * HID)
    gate_up_grad(1)
    gb_ = g2a(1)
    sum_wait(1, n_second)
    gacc[...] = jnp.zeros_like(gacc)

    def norm_two_back(i):
        r = i * 32
        gn = sum_rows(1, r, 32)
        v = mid[pl.ds(r, 32), :]
        inv = lax.rsqrt(jnp.mean(v * v, axis=1, keepdims=True) + NORM_EPSILON)
        unit = v * inv
        gacc[1:2, :] += jnp.sum(gn * unit, axis=0, keepdims=True)
        scaled = gn * sml[1:2, :]
        inner = jnp.mean(scaled * unit, axis=1, keepdims=True)
        out = cot[ty, tc, pl.ds(r, 32), :].astype(F32) + inv * (scaled - unit * inner)
        gmid[pl.ds(r, 32), :] = out
        rmid[ty, tc, pl.ds(r, 32), :] = out.astype(BF16)
        mid_c.push(i)

    mid_c = Pieces(rmid)
    loop(4, norm_two_back)
    gb_ = g2b(1, gb_)
    gate_up_grad(2)
    ge_ = g2a(2)
    gc_ = g1a(3, gc_)
    mid_c.relay()
    ge_ = g2b(2, ge_)
    mid_c.wait()

    pg = mm(rmid[...].reshape(ROWS, D), w[:, :, :, :, OUT_AT : OUT_AT + CH].reshape(D, CH))
    for q in range(2):
        lanes = slice(q * TILE, (q + 1) * TILE)
        own = at_lane(t * 2 + q, TILE)
        gate_b, gate_c, values = pj[0, :, lanes], pj[1, :, lanes], pj[2, :, lanes]
        mixed = gate_b * values
        gv = pg[:, lanes]
        grad_c = gv * conv[:, lanes]
        grad_conv = gv * gate_c
        one_grad, two_grad = grad_conv * masks[0], grad_conv * masks[1]
        gacc[2:3, own] = jnp.sum(grad_conv * mixed, axis=0, keepdims=True)
        gacc[3:4, own] = jnp.sum(one_grad * pltpu.roll(mixed, 1, 0), axis=0, keepdims=True)
        gacc[4:5, own] = jnp.sum(two_grad * pltpu.roll(mixed, 2, 0), axis=0, keepdims=True)
        grad_mixed = (
            taps(0, own) * grad_conv
            + taps(1, own) * pltpu.roll(one_grad, ROWS - 1, 0)
            + taps(2, own) * pltpu.roll(two_grad, ROWS - 2, 0)
        )
        for j, v in enumerate((grad_mixed * values, grad_c, grad_mixed * gate_b)):
            lo = j * CH + q * TILE
            gp[:, :, :, lo : lo + TILE] = v.astype(BF16).reshape(2, 2, BLOCK, TILE)

    i_second = sum_start(3, gp, 0, 3 * CH)

    def mix_grad(i):
        a = one[:, :, :, at_lane(i, CH)].reshape(ROWS, CH).T
        g[i, :, :, :, :OUT_AT] = wide(mm(a, gp[...].reshape(ROWS, 3 * CH)).astype(BF16))
        b = rmid[:, :, :, at_lane(i, CH)].reshape(ROWS, CH).T
        g[i, :, :, :, OUT_AT:GU_AT] = wide(mm(b, gated[...].reshape(ROWS, CH)).astype(BF16))

    loop(NZ, mix_grad)
    ga_ = g2a(0)

    def gain_one(i):
        lanes = at_lane(i, CH)
        out = jnp.zeros((1, CH), F32)
        for c, terms in ((1 - tc, ps), (tc, po)):
            for a in range(2):
                unit = tok[a, c, :, lanes].astype(F32) * jnp.tile(invs[a, c], (1, 2))
                out += jnp.sum(terms[3, i, a].astype(F32) * unit, axis=0, keepdims=True)
        gacc[0:1, lanes] = out

    loop(NZ, gain_one)
    for k in range(8):
        sgr[k // 2, k % 2] = gacc[:, k * TILE : (k + 1) * TILE]
    u_z = [
        links.push(sgr.at[zz], gr.at[i], to)
        for i, (zz, to) in enumerate(((zp, to_zp), (zo, to_zo), (zm, to_zm)))
    ]
    gb_ = g1a(1, gb_)
    gc_ = g1b(3, gc_)
    ga_ = g2b(0, ga_)
    arrived(u_z)
    sgr[z] = sgr[z] + gr[0] + gr[1] + gr[2]
    u_y = links.push(sgr.at[z, 1 - yh], gc.at[0], to_y)
    o_second = sum_start(2, hid, DOWN_AT, HID)
    ge_ = g1a(2, ge_)
    gb_ = g1b(1, gb_)
    u_y.wait_recv()
    gc[1] = sgr[z, yh] + gc[0]
    u_x = tile_send(gc.at[1], gc, 2, x_peers)
    sum_wait(3, i_second)

    def norm_one_back(i):
        r = i * 32
        gn = sum_rows(3, r, 32)
        unit = tok[ty, tc, pl.ds(r, 32), :].astype(F32)
        inv = lax.rsqrt(jnp.mean(unit * unit, axis=1, keepdims=True) + NORM_EPSILON)
        unit = unit * inv
        scaled = gn * sml[0:1, :]
        inner = jnp.mean(scaled * unit, axis=1, keepdims=True)
        tg[pl.ds(r, 32), :] = gmid[pl.ds(r, 32), :] + inv * (scaled - unit * inner)

    loop(4, norm_one_back)
    store(tg, tg_out)
    ga_ = g1_all(0, ga_)
    gc_ = gy(3, gc_)
    ge_ = g1b(2, ge_)
    gc[5] = tile_sum(gc[1], gc, 2, u_x)
    u_t = tile_send(gc.at[5], gc, 6, tensor_peers)
    gb_ = gy(1, gb_)
    sum_wait(2, o_second)

    def out_rows(i):
        r = i * 32
        bo[pl.ds(r, 32), :] = (mid[pl.ds(r, 32), :] + sum_rows(2, r, 32)).astype(BF16)

    loop(4, out_rows)
    store(bo, bo_out)
    ga_ = gy_all(0, ga_)
    gend(3, gc_)
    ge_ = gy(2, ge_)
    gend(1, gb_)
    gc[9] = pltpu.roll(tile_sum(gc[5], gc, 6, u_t), TILE - place, 1)
    for j in (1, 2):
        loads[0, j].wait()
    update(0, (), gc[9, 0:5, 0:8], RATE_SMALL)
    put(0)
    gend(2, ge_)
    gend(0, ga_)
    for c in links.open:
        c.wait_send()
    for c in stores:
        c.wait()


N_COPIES = 240


def train_call(lengths, tokens, cotangent, *state):
    anywhere = pl.BlockSpec(memory_space=pltpu.HBM)
    rows = (2, 2, BLOCK)
    weights = state[:5]
    out_shape = [jax.ShapeDtypeStruct((BLOCK, D), BF16), jax.ShapeDtypeStruct((BLOCK, D), F32)]
    for v in weights:
        out_shape += [jax.ShapeDtypeStruct(v.shape, F32)] * 3
    return pl.pallas_call(
        train_kernel,
        out_shape=out_shape,
        in_specs=[pl.BlockSpec(memory_space=pltpu.SMEM)] + [anywhere] * 17,
        out_specs=[anywhere] * 17,
        scratch_shapes=[pltpu.VMEM((3,) + v.shape, F32) for v in weights]
        + [
            pltpu.VMEM((BLOCK, D), BF16),
            pltpu.VMEM((BLOCK, D), F32),
            pltpu.SemaphoreType.DMA((40,)),
            pltpu.VMEM((NZ, NY, NX, SHARD, WIDE), BF16),
            pltpu.VMEM((NZ, NY, NX, SHARD, WIDE), BF16),
            pltpu.VMEM(rows + (D,), BF16),
            pltpu.VMEM(rows + (D,), BF16),
            pltpu.VMEM(rows + (D,), BF16),
            pltpu.VMEM(rows + (D,), BF16),
            pltpu.VMEM(rows + (D,), BF16),
            pltpu.VMEM((2, ROWS, TILE), F32),
            pltpu.VMEM((3, ROWS, CH), F32),
            pltpu.VMEM((ROWS, CH), F32),
            pltpu.VMEM(rows + (CH,), BF16),
            pltpu.VMEM(rows + (3 * CH,), BF16),
            pltpu.VMEM((TILES, ROWS, CH), F32),
            pltpu.VMEM(rows + (HID,), BF16),
            pltpu.VMEM(rows + (2 * HID,), BF16),
            pltpu.VMEM((BLOCK, D), F32),
            pltpu.VMEM((BLOCK, D), F32),
            pltpu.VMEM((8, D), F32),
            pltpu.VMEM((2, 8, TILE), F32),
            pltpu.VMEM((6, 8, TILE), F32),
            pltpu.VMEM((NZ, NY, 8, TILE), F32),
            pltpu.VMEM((NZ, NY, 8, TILE), F32),
            pltpu.VMEM((3, NY, 8, TILE), F32),
            pltpu.VMEM((10, 8, TILE), F32),
            pltpu.VMEM((8, D), F32),
            pltpu.VMEM(rows + (TILE,), F32),
            pltpu.VMEM((4, NZ, 2, BLOCK, CH), BF16),
            pltpu.VMEM((4, NZ, 2, BLOCK, CH), BF16),
            pltpu.VMEM((4, NZ, 2, BLOCK, CH), F32),
            pltpu.VMEM((4, NZ, BLOCK, CH), BF16),
            pltpu.VMEM((4, NZ, BLOCK, CH), BF16),
            pltpu.VMEM((2, 2, 4, HALF, WIDE), BF16),
            pltpu.VMEM((2, NY, NX, HALF, WIDE), BF16),
            pltpu.VMEM((2, NZ, NY, HALF, WIDE), BF16),
            pltpu.VMEM((2, 2, HALF, WIDE), BF16),
            pltpu.VMEM((2, 3, 2, HALF, WIDE), BF16),
            pltpu.VMEM((SHARD, WIDE), BF16),
            pltpu.SemaphoreType.DMA((N_COPIES,)),
            pltpu.SemaphoreType.DMA((N_COPIES,)),
        ],
        compiler_params=pltpu.CompilerParams(
            collective_id=0, has_side_effects=True, vmem_limit_bytes=63 * 1024 * 1024
        ),
        cost_estimate=pl.CostEstimate(
            flops=6 * ROWS * D * WIDE, bytes_accessed=8 * 1024 * 1024, transcendentals=ROWS * HID
        ),
    )(lengths, tokens, cotangent, *state)


def hand_over(*refs):
    n = (len(refs) - 2) // 3
    sources, targets, held = refs[:n], refs[n : 2 * n], refs[2 * n : 3 * n]
    load_sem, store_sem = refs[3 * n :]
    loads = [pltpu.make_async_copy(sources[i], held[i], load_sem.at[i]) for i in range(n)]
    stores = [pltpu.make_async_copy(held[i], targets[i], store_sem.at[i]) for i in range(n)]
    for c in loads:
        c.start()
    for i in range(n):
        loads[i].wait()
        stores[i].start()
    for c in stores:
        c.wait()


def per_device(
    tokens,
    cotangent,
    lengths,
    small,
    mix_in,
    mix_out,
    ffn_gate_up,
    ffn_down,
    small_first,
    small_second,
    in_first,
    in_second,
    out_first,
    out_second,
    gate_up_first,
    gate_up_second,
    down_first,
    down_second,
):
    found = train_call(
        lengths,
        tokens,
        cotangent,
        small,
        mix_in,
        mix_out,
        ffn_gate_up,
        ffn_down,
        small_first,
        small_second,
        in_first,
        in_second,
        out_first,
        out_second,
        gate_up_first,
        gate_up_second,
        down_first,
        down_second,
    )
    anywhere = pl.BlockSpec(memory_space=pltpu.HBM)
    n = len(found)
    return tuple(
        pl.pallas_call(
            hand_over,
            out_shape=[jax.ShapeDtypeStruct(v.shape, v.dtype) for v in found],
            in_specs=[anywhere] * n,
            out_specs=[anywhere] * n,
            scratch_shapes=[pltpu.VMEM(v.shape, v.dtype) for v in found]
            + [pltpu.SemaphoreType.DMA((n,))] * 2,
        )(*found)
    )


def solution(mesh):
    rows = P(("dp", "tensor"), None)
    small = P(None, ("dp", "tensor"))
    deep = P(None, "dp", "tensor")
    flat = P("dp", "tensor")
    in_specs = (rows, rows, P("dp", None), small, deep, flat, deep, flat)
    in_specs += (small,) * 2 + (deep,) * 2 + (flat,) * 2 + (deep,) * 2 + (flat,) * 2
    out_specs = (rows, rows) + (small,) * 3 + (deep,) * 3 + (flat,) * 3 + (deep,) * 3 + (flat,) * 3
    return jax.shard_map(
        per_device, mesh=mesh, in_specs=in_specs, out_specs=out_specs, check_vma=False
    )
```
